512 devices in a mesh: section: 16 (over z, x_hi), dp: 32 (over y, x_lo, core).
Axes of the slice: x: 4 (x_hi: 2, x_lo: 2; x = x_hi * 2 + x_lo), y: 8, z: 8, core: 2. Of those that a mesh axis runs over, the one named last changes fastest.
Arguments:
- acts: bfloat16 [16, 4096, 8192], P('section', 'dp'), may hold values from -1000 to 1000
- gain: float32 [16, 8192], P('section'), may hold values from 0.1 to 1.9
- kv_grad: bfloat16 [16, 4096, 256], P('section', 'dp'), may hold values from -6 to 6
- master: float32 [16, 8192, 256], P('section', 'dp'), may hold values from -0.0625 to 0.0625
- moment_one: float32 [16, 8192, 256], P('section', 'dp'), may hold values from -320 to 320
- moment_two: float32 [16, 8192, 256], P('section', 'dp'), may hold values from 1000 to 1000000
Outputs:
- new_master: float32 [16, 8192, 256], P('section', 'dp')
- new_moment_one: float32 [16, 8192, 256], P('section', 'dp')
- new_moment_two: float32 [16, 8192, 256], P('section', 'dp')
- input_grad: bfloat16 [4096, 8192], P('dp', 'section')
- kv_next: float32 [16, 4096, 256], P('section', 'dp')
The draws below stay inside these ranges and needn't reach their ends.
All inputs are finite; a program needn't handle non-finite values.
Results may differ from the reference program's by a relative error of at most 0.0049.
The reference program's roundings to bfloat16 on the way (of `hidden`, `weight_old`, `branch_grad` and `weight_new`) count: a program that leaves them out, or rounds other values in their place, can miss the bound.
Values may be sent and summed in bfloat16 or wider, within the bound.
A program may use at most 64 MiB of HBM per device.

```python
import math
import jax
import jax.numpy as jnp
from jax import lax

D = 8192
TOK_DEV = 128
STEP = 20
KV = 256
LAYERS = 16
TOKENS = 4096
N_DP = 32


def draw_acts(key, part):
    key = jax.random.fold_in(key, 11)
    key_base, key_rows, key_cols = jax.random.split(key, 3)
    shape = (LAYERS, TOKENS, D)
    base = jax.random.normal(key_base, shape, jnp.float32)
    base = jnp.clip(base, -6.0, 6.0)
    row_scale = jnp.exp(jax.random.uniform(key_rows, (LAYERS, TOKENS, 1), jnp.float32, 0.0, math.log(10.0)))
    col_scale = jnp.exp(jax.random.uniform(key_cols, (LAYERS, 1, D), jnp.float32, 0.0, math.log(10.0)))
    return (base * row_scale * col_scale).astype(jnp.bfloat16)


def block_levels(own_key, dims, pieces, smallest, top_value):
    level = 1.0
    for dim, shards_of in pieces:
        steps = jax.random.uniform(jax.random.fold_in(jax.random.fold_in(own_key, 6), dim), (shards_of,), jnp.float32, smallest / len(pieces), top_value / len(pieces))
        level = level * jnp.repeat(jnp.exp(steps), dims[dim] // shards_of).reshape((-1,) + (1,) * (len(dims) - 1 - dim))
    return level


def gaussian(own_key, extent, scale, most, shards=(), kind=jnp.bfloat16):
    level = block_levels(own_key, extent, shards, -0.22, 0.18) if shards else 1.0
    entries = jax.random.normal(own_key, extent, jnp.float32) * scale * level
    return jnp.minimum(jnp.maximum(entries, -most), most).astype(kind)


def setup_inputs(seed: int = 0) -> dict:
    streams_of = jax.random.split(jax.random.key(seed), 7)
    return {
        "acts": draw_acts(jax.random.fold_in(streams_of[6], 71), 0),
        "gain": jnp.clip(1.0 + 0.18 * jax.random.normal(streams_of[1], (LAYERS, D), jnp.float32), 0.1, 1.9),
        "kv_grad": gaussian(streams_of[2], (LAYERS, TOKENS, KV), 1.0, 6.0, ((0, 16), (1, 32))),
        "master": gaussian(streams_of[3], (LAYERS, D, KV), D ** -0.5, 0.0625, ((0, 16), (1, 32)), jnp.float32),
        "moment_one": gaussian(streams_of[4], (LAYERS, D, KV), 50.0, 320.0, ((0, 16), (1, 32)), jnp.float32),
        "moment_two": jnp.clip(jnp.exp(math.log(1000000) - 6.9077553 * jax.random.uniform(streams_of[5], (LAYERS, D, KV), jnp.float32) ** block_levels(streams_of[5], (LAYERS, D, KV), ((0, 16), (1, 32)), -0.2, 0.2)), 1000.0, 1000000),
    }


NORM_EPS = 1e-05
ADAM_EPS = 1e-08
BETA_ONE = 0.9
BETA_TWO = 0.95
LEARN_RATE = 0.00015
DECAY_RATE = 0.1

def normed(inputs, gain_row):
    values = inputs.astype(jnp.float32)
    root_mean = jnp.sqrt(lax.optimization_barrier(jnp.mean(values * values, axis=-1, keepdims=True)) + NORM_EPS)
    unit_rows = values / root_mean
    return (root_mean, unit_rows, (unit_rows * gain_row).astype(jnp.bfloat16))

def reference(acts, gain, kv_grad, master, moment_one, moment_two):
    running = jnp.zeros((TOKENS, D), jnp.float32)
    masters, firsts, seconds, nexts = ([], [], [], [])
    for layer in range(LAYERS):
        root_mean, unit_rows, hidden = normed(acts[layer], gain[layer])
        upstream = kv_grad[layer]
        weight_old = master[layer].astype(jnp.bfloat16)
        back_proj = jnp.dot(upstream, weight_old.T, preferred_element_type=jnp.float32)
        scaled = back_proj * gain[layer]
        branch_grad = (scaled - unit_rows * lax.optimization_barrier(jnp.mean(scaled * unit_rows, axis=-1, keepdims=True))) / root_mean
        rounded = lax.optimization_barrier(branch_grad.astype(jnp.bfloat16))
        running = running + rounded.astype(jnp.float32)

        def block_sum(carry, position):
            start = (position * TOK_DEV).astype(jnp.int32)
            block_rows = lax.dynamic_slice_in_dim(hidden, start, TOK_DEV, 0)
            block_up = lax.dynamic_slice_in_dim(upstream, start, TOK_DEV, 0)
            product = jnp.dot(block_rows.T, block_up, preferred_element_type=jnp.float32)
            product = lax.optimization_barrier(product.astype(jnp.bfloat16))
            return (carry + product.astype(jnp.float32), None)
        gradient, _ = lax.scan(block_sum, jnp.zeros((D, KV), jnp.float32), jnp.arange(N_DP, dtype=jnp.int32))
        first_new = BETA_ONE * moment_one[layer] + (1.0 - BETA_ONE) * gradient
        second_new = BETA_TWO * moment_two[layer] + (1.0 - BETA_TWO) * gradient * gradient
        direction = first_new / (1.0 - BETA_ONE ** STEP) / (jnp.sqrt(second_new / (1.0 - BETA_TWO ** STEP)) + ADAM_EPS)
        updated = master[layer] - LEARN_RATE * (direction + DECAY_RATE * master[layer])
        weight_new = updated.astype(jnp.bfloat16)
        nexts.append(jnp.dot(hidden, weight_new, preferred_element_type=jnp.float32))
        masters.append(updated)
        firsts.append(first_new)
        seconds.append(second_new)
    return (jnp.stack(masters), jnp.stack(firsts), jnp.stack(seconds), running.astype(jnp.bfloat16), jnp.stack(nexts))
```

```python
import jax
import jax.numpy as jnp
from jax import lax
from jax.experimental import pallas as pl
from jax.experimental.pallas import tpu as pltpu
from jax.sharding import PartitionSpec as P

STEP = 20
NORM_EPS = 1e-05
ADAM_EPS = 1e-08
BETA_ONE = 0.9
BETA_TWO = 0.95
LEARN_RATE = 0.00015
DECAY_RATE = 0.1

F32 = jnp.float32
BF16 = jnp.bfloat16
N = 8
D = 8192
TOK = 128
HALF = 64
W = 256
GATHER_ORDER = (0, 1, 7, 2, 6, 3, 5, 4)
SCATTER_ORDER = (4, 3, 5, 2, 6, 1, 7, 0)


def rows_of(half):
    return pl.ds(half * HALF, HALF)


def wide(a):
    return jnp.concatenate([a, a], axis=-1)


def kernel(
    acts, gain, kv, master, mom1, mom2,
    o_master, o_m1, o_m2, o_in, o_kv,
    a_full, gain_v, mas_v, m1_v, m2_v,
    xa, kvb, kvt, rmb, invc, wt, wn, hid, sc, macc, msend, mrecv, mcol,
    gfin, ysend, yrecv, zsend, zrecv, xsend, xrecv, kvn, knr,
    nm_v, n1_v, n2_v, oin_v, okv_v,
    l_in, l_acts, s_acts, r_acts, s_kv, r_kv, s_rm, r_rm, s_m, r_m,
    s_w, r_w, s_n, r_n, s_y, r_y, s_z, r_z, s_x, r_x, s_k, r_k, l_out,
):
    section = lax.axis_index("section")
    dp = lax.axis_index("dp")
    z = lax.div(section, 2)
    xh = lax.rem(section, 2)
    y = lax.div(dp, 4)
    q = lax.rem(dp, 4)
    xl = lax.div(q, 2)
    c = lax.rem(q, 2)
    mates = (xl * 2 + (1 - c), (1 - xl) * 2 + c, (1 - xl) * 2 + (1 - c))

    def ring(at, off):
        return lax.rem(at + off, N)

    def y_dev(off):
        return (section, ring(y, off) * 4 + q)

    def z_dev(off):
        return (ring(z, off) * 2 + xh, dp)

    def mate_dev(mate):
        return (section, y * 4 + mate)

    def remote(src, dst, send, recv, device):
        return pltpu.make_async_remote_copy(
            src_ref=src, dst_ref=dst, send_sem=send, recv_sem=recv,
            device_id=device, device_id_type=pl.DeviceIdType.MESH,
        )

    def wait_bytes(ref, sem):
        pltpu.make_async_copy(ref, ref, sem).wait()

    def columns(block):
        return pl.ds(pl.multiple_of(block * 1024 + q * W, W), W)

    loads = [
        pltpu.make_async_copy(master.at[0], mas_v, l_in.at[0]),
        pltpu.make_async_copy(acts.at[0], a_full, l_in.at[1]),
        pltpu.make_async_copy(kv.at[0], kvb.at[q], l_in.at[2]),
        pltpu.make_async_copy(gain, gain_v, l_in.at[3]),
        pltpu.make_async_copy(mom1.at[0], m1_v, l_in.at[4]),
        pltpu.make_async_copy(mom2.at[0], m2_v, l_in.at[5]),
    ]
    for load in loads:
        load.start()

    def own_acts(i):
        block = ring(y, GATHER_ORDER[i])
        return pltpu.make_async_copy(acts.at[0, :, columns(block)], xa.at[block, q], l_acts.at[i])

    for i in range(N):
        own_acts(i).start()

    barrier = pltpu.get_barrier_semaphore()
    for fh in range(2):
        for fl in range(2):
            for fc in range(2):
                if fh + fl + fc == 0:
                    continue
                other_h = 1 - xh if fh else xh
                other_l = 1 - xl if fl else xl
                other_c = 1 - c if fc else c
                pl.semaphore_signal(
                    barrier, inc=1, device_id=(z * 2 + other_h, y * 4 + other_l * 2 + other_c),
                    device_id_type=pl.DeviceIdType.MESH,
                )
    for device in (y_dev(1), y_dev(7), z_dev(1), z_dev(7)):
        pl.semaphore_signal(barrier, inc=1, device_id=device, device_id_type=pl.DeviceIdType.MESH)
    pl.semaphore_wait(barrier, 11)

    def send_acts(half, i):
        order = (GATHER_ORDER, SCATTER_ORDER)[half]
        block = ring(y, order[i])
        for mate in mates:
            source = acts.at[0, rows_of(half), pl.ds(pl.multiple_of(block * 1024 + mate * W, W), W)]
            remote(source, xa.at[block, q, rows_of(half)], s_acts.at[half, i], r_acts.at[half, i], mate_dev(mate)).start()

    def wait_acts(half, i):
        if half == 0:
            own_acts(i).wait()
        wait_bytes(xa.at[0, pl.ds(0, 3), rows_of(0)], r_acts.at[half, i])

    for mate in mates:
        remote(kv.at[0], kvb.at[q], s_kv, r_kv, mate_dev(mate)).start()
    send_acts(0, 0)
    send_acts(0, 1)

    def gather_copy(buffer, send, recv, way, hop):
        off = N - hop if way == 0 else hop
        block = buffer.at[ring(y, off)]
        if hop == 3:
            block = block.at[pl.ds(way * 128, 128)]
        return remote(block, block, send.at[way, hop], recv.at[way, hop], y_dev(1 if way == 0 else 7))

    def gather_hop(buffer, send, recv, hop):
        for way in range(2):
            if hop > 0:
                gather_copy(buffer, send, recv, way, hop - 1).wait_recv()
            if hop < 4:
                gather_copy(buffer, send, recv, way, hop).start()

    loads[0].wait()
    wt[y] = jnp.transpose(mas_v[...]).astype(BF16)
    gather_hop(wt, s_w, r_w, 0)

    loads[1].wait()

    def add_squares(step, total):
        part = a_full[:, pl.ds(pl.multiple_of(step * 512, 512), 512)].astype(F32)
        part = part * part
        return total + ((part[:, :128] + part[:, 128:256]) + (part[:, 256:384] + part[:, 384:]))

    squares = lax.fori_loop(0, 16, add_squares, jnp.zeros((TOK, 128), F32))
    mean_row = jnp.sum(jnp.transpose(squares), axis=0, keepdims=True) / D
    rmb[q] = jnp.broadcast_to(jnp.sqrt(mean_row + NORM_EPS), (8, 128))
    for mate in mates:
        remote(rmb.at[q], rmb.at[q], s_rm, r_rm, mate_dev(mate)).start()
    for i in range(2, N):
        send_acts(0, i)

    for load in loads[2:4]:
        load.wait()
    wait_bytes(kvb.at[pl.ds(0, 3)], r_kv)
    wait_bytes(rmb.at[pl.ds(0, 3)], r_rm)

    def prepare(slot, carry):
        root = jnp.transpose(jnp.broadcast_to(rmb[slot][0:1, :], (128, 128)))
        invc[slot] = 1.0 / root
        kvt[slot] = jnp.transpose(kvb[slot].astype(F32)).astype(BF16)
        return carry

    lax.fori_loop(0, 4, prepare, 0)

    def forward(half, block):
        gain_row = gain_v[:, columns(block)]
        back = jnp.dot(
            kvb[:, rows_of(half), :].reshape(4 * HALF, W), wt[block], preferred_element_type=F32
        )
        sc[block, :, rows_of(half), :] = back.reshape(4, HALF, W)

        def one(slot, carry):
            unit = xa[block, slot, rows_of(half), :].astype(F32) * wide(invc[slot, rows_of(half), :])
            hid[block, slot, rows_of(half), :] = (unit * gain_row).astype(BF16)
            scaled = sc[block, slot, rows_of(half), :] * gain_row
            sc[block, slot, rows_of(half), :] = scaled
            product = scaled * unit
            macc[half, slot] += product[:, :128] + product[:, 128:]
            return carry

        lax.fori_loop(0, 4, one, 0)

    def send_means(half):
        msend[half] = jnp.zeros((8, 128), F32)
        for pair in range(2):
            both = macc[half, pl.ds(pair * 2, 2)].reshape(128, 128)
            msend[half, pair : pair + 1, :] = jnp.sum(jnp.transpose(both), axis=0, keepdims=True)
        for r, mate in enumerate(mates):
            remote(msend.at[half], mrecv.at[half, r], s_m.at[half, r], r_m.at[half, r], mate_dev(mate)).start()

    def get_means(half):
        for r, mate in enumerate(mates):
            remote(msend.at[half], mrecv.at[half, r], s_m.at[half, r], r_m.at[half, r], mate_dev(mate)).wait_recv()
        total = ((msend[half] + mrecv[half, 0]) + (mrecv[half, 1] + mrecv[half, 2])) / D
        for pair in range(2):
            column = jnp.transpose(jnp.broadcast_to(total[pair : pair + 1, :], (128, 128)))
            mcol[half, pl.ds(pair * 2, 2)] = column.reshape(2, HALF, 128)

    def branch(half, block, slot):
        inv = wide(invc[slot, rows_of(half), :])
        unit = xa[block, slot, rows_of(half), :].astype(F32) * inv
        return ((sc[block, slot, rows_of(half), :] - unit * wide(mcol[half, slot])) * inv).astype(BF16)

    def z_copy(half, way, step):
        part = pl.ds(2 * way, 2) if step == 0 else pl.ds(0, 4)
        return remote(
            zsend.at[half, way, step, part], zrecv.at[half, way, step, part],
            s_z.at[half, way, step], r_z.at[half, way, step], z_dev(1 if way == 0 else 7),
        )

    def z_step(half, step):
        if step == 0:
            block = ring(z, 4)
            for way in range(2):
                for slot in (2 * way, 2 * way + 1):
                    zsend[half, way, 0, slot] = branch(half, block, slot)
                z_copy(half, way, 0).start()
            return
        for way in range(2):
            z_copy(half, way, step - 1).wait_recv()
            block = ring(z, 4 - step if way == 0 else 4 + step)

            def one(slot, carry):
                own = branch(half, block, slot).astype(F32)
                zsend[half, way, step, slot] = (own + zrecv[half, way, step - 1, slot].astype(F32)).astype(BF16)
                return carry

            if step == 1:
                for slot in range(4):
                    if slot // 2 == way:
                        one(slot, 0)
                    else:
                        zsend[half, way, step, slot] = branch(half, block, slot)
            else:
                lax.fori_loop(0, 4, one, 0)
            z_copy(half, way, step).start()

    x_section = z * 2 + xl
    x_source = xh * 2 + c

    def x_copy(half, slot):
        return remote(
            xsend.at[half, slot], xrecv.at[half, x_source], s_x.at[half, slot], r_x.at[half, x_source],
            (x_section, y * 4 + slot),
        )

    def stays(slot):
        return jnp.logical_and(xh == xl, q == slot)

    def z_last(half):
        for way in range(2):
            z_copy(half, way, 3).wait_recv()

        def one(slot, carry):
            total = branch(half, z, slot).astype(F32)
            total = total + (zrecv[half, 0, 3, slot].astype(F32) + zrecv[half, 1, 3, slot].astype(F32))
            xsend[half, slot] = total.astype(BF16)
            return carry

        lax.fori_loop(0, 4, one, 0)
        for slot in range(4):
            @pl.when(stays(slot))
            def _():
                pltpu.make_async_copy(xsend.at[half, slot], xrecv.at[half, x_source], r_x.at[half, x_source]).start()

            @pl.when(jnp.logical_not(stays(slot)))
            def _():
                x_copy(half, slot).start()

    def x_last(half):
        for source in range(4):
            wait_bytes(xrecv.at[half, source], r_x.at[half, source])
        for col in range(2):
            total = xrecv[half, col].astype(F32) + xrecv[half, 2 + col].astype(F32)
            oin_v[rows_of(half), col * W : (col + 1) * W] = total.astype(BF16)

    macc[...] = jnp.zeros_like(macc)
    for i in range(N):
        send_acts(1, i)
        if i in (1, 3, 5, 7):
            gather_hop(wt, s_w, r_w, (i + 1) // 2)
        wait_acts(0, i)
        forward(0, ring(y, GATHER_ORDER[i]))
    send_means(0)

    def y_copy(way, step):
        part = pl.ds(way * 128, 128) if step == 0 else pl.ds(0, W)
        return remote(
            ysend.at[way, step, part], yrecv.at[way, step, part], s_y.at[way, step], r_y.at[way, step],
            y_dev(1 if way == 0 else 7),
        )

    for i in range(N):
        if i == 0:
            get_means(0)
        if i % 2 == 0:
            z_step(0, i // 2)
        off = SCATTER_ORDER[i]
        block = ring(y, off)
        wait_acts(1, i)
        forward(1, block)
        total = None
        for slot in range(4):
            product = jnp.dot(kvt[slot], hid[block, slot], preferred_element_type=F32).astype(BF16).astype(F32)
            total = product if total is None else total + product
        if off == 4:
            ysend[0, 0] = total.astype(BF16)
            ysend[1, 0] = total.astype(BF16)
            for way in range(2):
                y_copy(way, 0).start()
        elif off == 0:
            for way in range(2):
                y_copy(way, 3).wait_recv()
            gfin[...] = total + (yrecv[0, 3].astype(F32) + yrecv[1, 3].astype(F32))
        else:
            way = 0 if off < 4 else 1
            step = 4 - off if off < 4 else off - 4
            y_copy(way, step - 1).wait_recv()
            got = yrecv[way, step - 1]
            if step == 1:
                ysend[way, 1] = total.astype(BF16)
                mine = slice(way * 128, way * 128 + 128)
                ysend[way, 1, mine, :] = (total[mine] + got[mine].astype(F32)).astype(BF16)
            else:
                ysend[way, step] = (total + got.astype(F32)).astype(BF16)
            y_copy(way, step).start()
    send_means(1)

    for load in loads[4:6]:
        load.wait()
    gradient = jnp.transpose(gfin[...])
    old = mas_v[...]
    first_new = BETA_ONE * m1_v[...] + (1.0 - BETA_ONE) * gradient
    second_new = BETA_TWO * m2_v[...] + (1.0 - BETA_TWO) * gradient * gradient
    direction = (
        first_new / (1.0 - BETA_ONE**STEP) / (jnp.sqrt(second_new / (1.0 - BETA_TWO**STEP)) + ADAM_EPS)
    )
    updated = old - LEARN_RATE * (direction + DECAY_RATE * old)
    wn[y] = updated.astype(BF16)
    gather_hop(wn, s_n, r_n, 0)
    nm_v[...] = updated
    n1_v[...] = first_new
    n2_v[...] = second_new
    stores = [
        pltpu.make_async_copy(nm_v, o_master.at[0], l_out.at[0]),
        pltpu.make_async_copy(n1_v, o_m1.at[0], l_out.at[1]),
        pltpu.make_async_copy(n2_v, o_m2.at[0], l_out.at[2]),
    ]
    for store in stores:
        store.start()

    def next_part(off, first=False):
        block = ring(y, off)
        part = jnp.dot(hid[block].reshape(4 * TOK, W), wn[block], preferred_element_type=F32).reshape(4, TOK, W)
        kvn[...] = part if first else kvn[...] + part

    z_last(0)
    get_means(1)
    z_step(1, 0)
    next_part(0, True)
    gather_hop(wn, s_n, r_n, 1)
    z_step(1, 1)
    next_part(1)
    next_part(7)
    gather_hop(wn, s_n, r_n, 2)
    x_last(0)
    next_part(2)
    next_part(6)
    z_step(1, 2)
    gather_hop(wn, s_n, r_n, 3)
    next_part(3)
    next_part(5)
    gather_hop(wn, s_n, r_n, 4)
    next_part(4)

    def next_copy(r, mate):
        return remote(kvn.at[mate], knr.at[r], s_k.at[r], r_k.at[r], mate_dev(mate))

    for r, mate in enumerate(mates):
        next_copy(r, mate).start()
    z_step(1, 3)
    for r, mate in enumerate(mates):
        next_copy(r, mate).wait_recv()
    okv_v[...] = (kvn[q] + knr[0]) + (knr[1] + knr[2])
    stores.append(pltpu.make_async_copy(okv_v, o_kv.at[0], l_out.at[3]))
    stores[-1].start()
    z_last(1)
    x_last(1)
    stores.append(pltpu.make_async_copy(oin_v, o_in, l_out.at[4]))
    stores[-1].start()

    wait_bytes(kvb.at[pl.ds(0, 3)], s_kv)
    wait_bytes(rmb.at[pl.ds(0, 3)], s_rm)
    for half in range(2):
        for i in range(N):
            wait_bytes(xa.at[0, pl.ds(0, 3), rows_of(0)], s_acts.at[half, i])
        for r, mate in enumerate(mates):
            remote(msend.at[half], mrecv.at[half, r], s_m.at[half, r], r_m.at[half, r], mate_dev(mate)).wait_send()
        for way in range(2):
            for step in range(4):
                z_copy(half, way, step).wait_send()
        for slot in range(4):
            @pl.when(jnp.logical_not(stays(slot)))
            def _():
                x_copy(half, slot).wait_send()
    for way in range(2):
        for step in range(4):
            gather_copy(wt, s_w, r_w, way, step).wait_send()
            gather_copy(wn, s_n, r_n, way, step).wait_send()
            y_copy(way, step).wait_send()
    for r, mate in enumerate(mates):
        next_copy(r, mate).wait_send()
    for store in stores:
        store.wait()


def per_device(acts, gain, kv_grad, master, moment_one, moment_two):
    anywhere = pl.BlockSpec(memory_space=pl.ANY)
    vmem = pltpu.VMEM
    dma = pltpu.SemaphoreType.DMA
    rows = jax.ShapeDtypeStruct((1, W, W), F32)
    scratch = [
        vmem((TOK, D), BF16),
        vmem((1, D), F32),
        vmem((W, W), F32), vmem((W, W), F32), vmem((W, W), F32),
        vmem((N, 4, TOK, W), BF16),
        vmem((4, TOK, W), BF16),
        vmem((4, W, TOK), BF16),
        vmem((4, 8, 128), F32),
        vmem((4, TOK, 128), F32),
        vmem((N, W, W), BF16),
        vmem((N, W, W), BF16),
        vmem((N, 4, TOK, W), BF16),
        vmem((N, 4, TOK, W), F32),
        vmem((2, 4, HALF, 128), F32),
        vmem((2, 8, 128), F32),
        vmem((2, 3, 8, 128), F32),
        vmem((2, 4, HALF, 128), F32),
        vmem((W, W), F32),
        vmem((2, 4, W, W), BF16), vmem((2, 4, W, W), BF16),
        vmem((2, 2, 4, 4, HALF, W), BF16), vmem((2, 2, 4, 4, HALF, W), BF16),
        vmem((2, 4, HALF, W), BF16), vmem((2, 4, HALF, W), BF16),
        vmem((4, TOK, W), F32),
        vmem((3, TOK, W), F32),
        vmem((W, W), F32), vmem((W, W), F32), vmem((W, W), F32),
        vmem((TOK, 2 * W), BF16),
        vmem((TOK, W), F32),
        dma((6,)), dma((N,)), dma((2, N)), dma((2, N)),
        dma, dma, dma, dma,
        dma((2, 3)), dma((2, 3)),
        dma((2, 4)), dma((2, 4)), dma((2, 4)), dma((2, 4)),
        dma((2, 4)), dma((2, 4)),
        dma((2, 2, 4)), dma((2, 2, 4)),
        dma((2, 4)), dma((2, 4)),
        dma((3,)), dma((3,)), dma((5,)),
    ]
    return pl.pallas_call(
        kernel,
        out_shape=(
            rows, rows, rows,
            jax.ShapeDtypeStruct((TOK, 2 * W), BF16),
            jax.ShapeDtypeStruct((1, TOK, W), F32),
        ),
        in_specs=[anywhere] * 6,
        out_specs=(anywhere,) * 5,
        scratch_shapes=scratch,
        compiler_params=pltpu.CompilerParams(
            collective_id=0, has_side_effects=True, vmem_limit_bytes=48 * 1024 * 1024
        ),
        cost_estimate=pl.CostEstimate(flops=1_700_000_000, bytes_accessed=6_000_000, transcendentals=200_000),
    )(acts, gain, kv_grad, master, moment_one, moment_two)


def solution(mesh):
    placed = (
        P("section", "dp", None),
        P("section", None),
        P("section", "dp", None),
        P("section", "dp", None),
        P("section", "dp", None),
        P("section", "dp", None),
    )
    return jax.shard_map(
        per_device,
        mesh=mesh,
        in_specs=placed,
        out_specs=(
            P("section", "dp", None),
            P("section", "dp", None),
            P("section", "dp", None),
            P("dp", "section"),
            P("section", "dp", None),
        ),
        check_vma=False,
    )
```

```python
import contextlib

import jax
import jax.numpy as jnp
from jax import lax
from jax.experimental import pallas as pl
from jax.experimental.pallas import tpu as pltpu
from jax.sharding import PartitionSpec as P

STEP = 20
NORM_EPS = 1e-05
ADAM_EPS = 1e-08
BETA_ONE = 0.9
BETA_TWO = 0.95
LEARN_RATE = 0.00015
DECAY_RATE = 0.1

F32 = jnp.float32
BF16 = jnp.bfloat16
N = 8
D = 8192
TOK = 128
HALF = 64
VMEM_BYTES = 64 * 1024 * 1024
W = 256
SETS = (
    (0, 4), (1, 4), (0, 3), (1, 3), (0, 5), (1, 5), (0, 2), (0, 6),
    (0, 1), (0, 7), (0, 0), (1, 2), (1, 6), (1, 1), (1, 7), (1, 0),
)


def part_of(name):
    return contextlib.nullcontext()


def rows_of(half):
    return pl.ds(half * HALF, HALF)


def wide(a):
    return jnp.concatenate([a, a], axis=-1)


def kernel(
    acts, gain, kv, master, mom1, mom2,
    o_master, o_m1, o_m2, o_in, o_kv,
    a_full, gain_v, mas_v, m1_v, m2_v,
    xa, kvb, kvt, rmb, invc, wt, wn, hid, sc, macc, msend, mrecv, mcol,
    gsum, ysend, yrecv, zsend, zrecv, xsend, xrecv, kvn, kvs, knr, kns,
    nm_v, n1_v, n2_v, oin_v, okv_v,
    l_in, l_acts, s_acts, r_acts, s_kv, r_kv, s_rm, r_rm, s_m, r_m,
    s_w, r_w, s_n, r_n, s_y, r_y, s_z, r_z, s_x, r_x, s_k, r_k, l_out,
):
    section = lax.axis_index("section")
    dp = lax.axis_index("dp")
    z = lax.div(section, 2)
    xh = lax.rem(section, 2)
    y = lax.div(dp, 4)
    q = lax.rem(dp, 4)
    xl = lax.div(q, 2)
    c = lax.rem(q, 2)
    mates = (xl * 2 + (1 - c), (1 - xl) * 2 + c, (1 - xl) * 2 + (1 - c))

    def ring(at, off):
        return lax.rem(at + off, N)

    def y_dev(off):
        return (section, ring(y, off) * 4 + q)

    def z_dev(off):
        return (ring(z, off) * 2 + xh, dp)

    def mate_dev(mate):
        return (section, y * 4 + mate)

    def remote(src, dst, send, recv, device):
        return pltpu.make_async_remote_copy(
            src_ref=src, dst_ref=dst, send_sem=send, recv_sem=recv,
            device_id=device, device_id_type=pl.DeviceIdType.MESH,
        )

    def wait_bytes(ref, sem):
        pltpu.make_async_copy(ref, ref, sem).wait()

    def columns(block):
        return pl.ds(pl.multiple_of(block * 1024 + q * W, W), W)

    loads = [
        pltpu.make_async_copy(master.at[0], mas_v, l_in.at[0]),
        pltpu.make_async_copy(acts.at[0], a_full, l_in.at[1]),
        pltpu.make_async_copy(kv.at[0], kvb.at[q], l_in.at[2]),
        pltpu.make_async_copy(gain, gain_v, l_in.at[3]),
        pltpu.make_async_copy(mom1.at[0], m1_v, l_in.at[4]),
        pltpu.make_async_copy(mom2.at[0], m2_v, l_in.at[5]),
    ]
    for load in loads:
        load.start()

    def own_acts(off):
        block = ring(y, off)
        return pltpu.make_async_copy(acts.at[0, :, columns(block)], xa.at[block, q], l_acts.at[off])

    for off in range(N):
        own_acts(off).start()

    barrier = pltpu.get_barrier_semaphore()
    for fh in range(2):
        for fl in range(2):
            for fc in range(2):
                if fh + fl + fc == 0:
                    continue
                other_h = 1 - xh if fh else xh
                other_l = 1 - xl if fl else xl
                other_c = 1 - c if fc else c
                pl.semaphore_signal(
                    barrier, inc=1, device_id=(z * 2 + other_h, y * 4 + other_l * 2 + other_c),
                    device_id_type=pl.DeviceIdType.MESH,
                )
    for device in (y_dev(1), y_dev(7), z_dev(1), z_dev(7)):
        pl.semaphore_signal(barrier, inc=1, device_id=device, device_id_type=pl.DeviceIdType.MESH)

    with part_of("barrier"):
        pl.semaphore_wait(barrier, 11)

    def send_acts(k):
        half, off = SETS[k]
        block = ring(y, off)
        for mate in mates:
            source = acts.at[0, rows_of(half), pl.ds(pl.multiple_of(block * 1024 + mate * W, W), W)]
            remote(source, xa.at[block, q, rows_of(half)], s_acts.at[k], r_acts.at[k], mate_dev(mate)).start()

    def wait_acts(k):
        half, off = SETS[k]
        if half == 0:
            own_acts(off).wait()
        wait_bytes(xa.at[0, pl.ds(0, 3), rows_of(0)], r_acts.at[k])

    def gather_copy(buffer, send, recv, way, hop, part):
        off = N - hop if way == 0 else hop
        block = buffer.at[ring(y, off), pl.ds(part * 128, 128)]
        return remote(block, block, send.at[way, hop, part], recv.at[way, hop, part], y_dev(1 if way == 0 else 7))

    def gather_hop(buffer, send, recv, hop):
        for k in range(2):
            for way in range(2):
                part = k if way == 0 else 1 - k
                if hop > 0 and (hop < 4 or k == 0):
                    gather_copy(buffer, send, recv, way, hop - 1, part).wait_recv()
                if hop < 3 or (hop == 3 and k == 0):
                    gather_copy(buffer, send, recv, way, hop, part).start()

    def kv_copy(which):
        slot, device = ((q, mates[0]), (q, mates[1]), (mates[1], mates[0]))[which]
        return remote(kvb.at[slot], kvb.at[slot], s_kv.at[which], r_kv.at[which], mate_dev(device))

    loads[2].wait()
    kv_copy(1).start()
    kv_copy(0).start()
    send_acts(0)
    send_acts(1)
    with part_of("wt"):
        loads[0].wait()
        wt[y] = jnp.transpose(mas_v[...]).astype(BF16)
    gather_hop(wt, s_w, r_w, 0)

    with part_of("squares"):
        loads[1].wait()

        def add_squares(step, total):
            part = a_full[:, pl.ds(pl.multiple_of(step * 512, 512), 512)].astype(F32)
            part = part * part
            return total + ((part[:, :128] + part[:, 128:256]) + (part[:, 256:384] + part[:, 384:]))

        squares = lax.fori_loop(0, 16, add_squares, jnp.zeros((TOK, 128), F32))
        mean_row = jnp.sum(jnp.transpose(squares), axis=0, keepdims=True) / D
        rmb[q] = jnp.broadcast_to(jnp.sqrt(mean_row + NORM_EPS), (8, 128))
    for mate in mates:
        remote(rmb.at[q], rmb.at[q], s_rm, r_rm, mate_dev(mate)).start()
    for k in range(2, 11):
        send_acts(k)
    macc[...] = jnp.zeros_like(macc)
    loads[3].wait()

    with part_of("kv_wait"):
        kv_copy(1).wait_recv()
        kv_copy(2).start()
    with part_of("old_hop1"):
        gather_hop(wt, s_w, r_w, 1)
    with part_of("kv_wait"):
        kv_copy(0).wait_recv()
        kv_copy(2).wait_recv()
    with part_of("rm_wait"):
        wait_bytes(rmb.at[pl.ds(0, 3)], r_rm)

    def prepare(slot, carry):
        root = jnp.transpose(jnp.broadcast_to(rmb[slot][0:1, :], (128, 128)))
        invc[slot] = 1.0 / root
        kvt[slot] = jnp.transpose(kvb[slot].astype(F32)).astype(BF16)
        return carry

    with part_of("prepare"):
        lax.fori_loop(0, 4, prepare, 0)

    def hide(half, block):
        gain_row = gain_v[:, columns(block)]

        def one(slot, carry):
            unit = xa[block, slot, rows_of(half), :].astype(F32) * wide(invc[slot, rows_of(half), :])
            hid[block, slot, rows_of(half), :] = (unit * gain_row).astype(BF16)
            return carry

        lax.fori_loop(0, 4, one, 0)

    def back(half, block):
        gain_row = gain_v[:, columns(block)]
        product = jnp.dot(
            kvb[:, rows_of(half), :].reshape(4 * HALF, W), wt[block], preferred_element_type=F32
        )
        sc[block, :, rows_of(half), :] = product.reshape(4, HALF, W)

        def one(slot, carry):
            unit = xa[block, slot, rows_of(half), :].astype(F32) * wide(invc[slot, rows_of(half), :])
            scaled = sc[block, slot, rows_of(half), :] * gain_row
            sc[block, slot, rows_of(half), :] = scaled
            both = scaled * unit
            macc[half, slot] += both[:, :128] + both[:, 128:]
            return carry

        lax.fori_loop(0, 4, one, 0)

    def send_means(half):
        msend[half] = jnp.zeros((8, 128), F32)
        for pair in range(2):
            both = macc[half, pl.ds(pair * 2, 2)].reshape(128, 128)
            msend[half, pair : pair + 1, :] = jnp.sum(jnp.transpose(both), axis=0, keepdims=True)
        for r, mate in enumerate(mates):
            remote(msend.at[half], mrecv.at[half, r], s_m.at[half, r], r_m.at[half, r], mate_dev(mate)).start()

    def get_means(half):
        for r, mate in enumerate(mates):
            remote(msend.at[half], mrecv.at[half, r], s_m.at[half, r], r_m.at[half, r], mate_dev(mate)).wait_recv()
        total = ((msend[half] + mrecv[half, 0]) + (mrecv[half, 1] + mrecv[half, 2])) / D
        for pair in range(2):
            column = jnp.transpose(jnp.broadcast_to(total[pair : pair + 1, :], (128, 128)))
            mcol[half, pl.ds(pair * 2, 2)] = column.reshape(2, HALF, 128)

    def branch(half, block, slot):
        inv = wide(invc[slot, rows_of(half), :])
        unit = xa[block, slot, rows_of(half), :].astype(F32) * inv
        return ((sc[block, slot, rows_of(half), :] - unit * wide(mcol[half, slot])) * inv).astype(BF16)

    def z_copy(half, way, step, part):
        slots = pl.ds(2 * part, 2)
        return remote(
            zsend.at[half, way, step, slots], zrecv.at[half, way, step, slots],
            s_z.at[half, way, step, part], r_z.at[half, way, step, part], z_dev(1 if way == 0 else 7),
        )

    def z_step(half, step):
        for k in range(2):
            for way in range(2):
                part = 1 - way if k == 0 else way
                if step == 0 and k == 0:
                    continue
                block = ring(z, 4 - step if way == 0 else 4 + step)
                adds = step > 1 or (step == 1 and part == way)
                if adds:
                    z_copy(half, way, step - 1, part).wait_recv()
                for slot in (2 * part, 2 * part + 1):
                    own = branch(half, block, slot)
                    if adds:
                        own = (own.astype(F32) + zrecv[half, way, step - 1, slot].astype(F32)).astype(BF16)
                    zsend[half, way, step, slot] = own
                z_copy(half, way, step, part).start()

    x_section = z * 2 + xl
    x_source = xh * 2 + c

    def x_copy(half, slot):
        return remote(
            xsend.at[half, slot], xrecv.at[half, x_source], s_x.at[half, slot], r_x.at[half, x_source],
            (x_section, y * 4 + slot),
        )

    def stays(slot):
        return jnp.logical_and(xh == xl, q == slot)

    def z_last(half):
        for way in range(2):
            for part in range(2):
                z_copy(half, way, 3, part).wait_recv()

        def one(slot, carry):
            total = branch(half, z, slot).astype(F32)
            total = total + (zrecv[half, 0, 3, slot].astype(F32) + zrecv[half, 1, 3, slot].astype(F32))
            xsend[half, slot] = total.astype(BF16)
            return carry

        lax.fori_loop(0, 4, one, 0)
        for slot in range(4):
            @pl.when(stays(slot))
            def _():
                pltpu.make_async_copy(xsend.at[half, slot], xrecv.at[half, x_source], r_x.at[half, x_source]).start()

            @pl.when(jnp.logical_not(stays(slot)))
            def _():
                x_copy(half, slot).start()

    def x_last(half):
        for source in range(4):
            wait_bytes(xrecv.at[half, source], r_x.at[half, source])
        for col in range(2):
            total = xrecv[half, col].astype(F32) + xrecv[half, 2 + col].astype(F32)
            oin_v[rows_of(half), col * W : (col + 1) * W] = total.astype(BF16)

    def old_hop(hop):
        with part_of("old_hop%d" % hop):
            gather_hop(wt, s_w, r_w, hop)

    def new_hop(hop):
        with part_of("new_hop%d" % hop):
            gather_hop(wn, s_n, r_n, hop)

    def arrive(k):
        with part_of("acts_wait%d" % k):
            wait_acts(k)
        with part_of("hide"):
            half, off = SETS[k]
            hide(half, ring(y, off))

    def backs(*pairs):
        with part_of("back"):
            for half, off in pairs:
                back(half, ring(y, off))

    def grad(off):
        with part_of("grad"):
            block = ring(y, off)
            total = None
            for slot in range(4):
                product = jnp.dot(kvt[slot], hid[block, slot], preferred_element_type=F32).astype(BF16).astype(F32)
                total = product if total is None else total + product
            gsum[block] = total

    def means(half):
        with part_of("means%d" % half):
            get_means(half)

    def z_part(half, step):
        with part_of("z%d_%d" % (half, step)):
            if step < 4:
                z_step(half, step)
            else:
                z_last(half)

    def x_part(half):
        with part_of("x%d" % half):
            x_last(half)

    def y_copy(way, step, part):
        rows = pl.ds(part * 128, 128)
        return remote(
            ysend.at[way, step, rows], yrecv.at[way, step, rows], s_y.at[way, step, part], r_y.at[way, step, part],
            y_dev(1 if way == 0 else 7),
        )

    def y_step(step):
        for k in range(2):
            for way in range(2):
                part = 1 - way if k == 0 else way
                if step == 0 and k == 0:
                    continue
                block = ring(y, 4 - step if way == 0 else 4 + step)
                rows = pl.ds(part * 128, 128)
                total = gsum[block, rows]
                if step > 1 or (step == 1 and part == way):
                    y_copy(way, step - 1, part).wait_recv()
                    total = total + yrecv[way, step - 1, rows].astype(F32)
                ysend[way, step, rows] = total.astype(BF16)
                y_copy(way, step, part).start()

    def y_part(step):
        with part_of("y%d" % step):
            if step < 4:
                y_step(step)
                return
            for part in range(2):
                for way in range(2):
                    y_copy(way, 3, part).wait_recv()

    def next_part(off):
        with part_of("next"):
            block = ring(y, off)
            part = jnp.dot(hid[block].reshape(4 * TOK, W), wn[block], preferred_element_type=F32).reshape(4, TOK, W)
            kvn[...] = part if off == 0 else kvn[...] + part

    arrive(0)
    arrive(1)
    grad(4)
    arrive(2)
    arrive(3)
    old_hop(2)
    y_part(0)
    arrive(4)
    arrive(5)
    grad(3)
    grad(5)
    old_hop(3)
    y_part(1)
    send_acts(11)
    send_acts(12)
    backs((0, 3), (1, 3), (0, 5), (1, 5))
    arrive(6)
    backs((0, 2))
    arrive(7)
    backs((0, 6))
    arrive(8)
    backs((0, 1))
    old_hop(4)
    backs((0, 4), (1, 4))
    arrive(9)
    backs((0, 7))
    arrive(10)
    backs((0, 0))
    send_means(0)
    for k in range(13, 16):
        send_acts(k)
    arrive(11)
    backs((1, 2))
    grad(2)
    arrive(12)
    backs((1, 6))
    grad(6)
    y_part(2)
    means(0)
    z_part(0, 0)
    arrive(13)
    backs((1, 1))
    grad(1)
    arrive(14)
    backs((1, 7))
    grad(7)
    arrive(15)
    backs((1, 0))
    send_means(1)
    y_part(3)
    grad(0)
    z_part(0, 1)
    means(1)
    z_part(1, 0)
    y_part(4)

    with part_of("adam"):
        for load in loads[4:6]:
            load.wait()
        gradient = jnp.transpose(gsum[y] + (yrecv[0, 3].astype(F32) + yrecv[1, 3].astype(F32)))
        old = mas_v[...]
        first_new = BETA_ONE * m1_v[...] + (1.0 - BETA_ONE) * gradient
        second_new = BETA_TWO * m2_v[...] + (1.0 - BETA_TWO) * gradient * gradient
        direction = (
            first_new / (1.0 - BETA_ONE**STEP) / (jnp.sqrt(second_new / (1.0 - BETA_TWO**STEP)) + ADAM_EPS)
        )
        updated = old - LEARN_RATE * (direction + DECAY_RATE * old)
        wn[y] = updated.astype(BF16)
        new_hop(0)
        nm_v[...] = updated
        n1_v[...] = first_new
        n2_v[...] = second_new
    stores = [
        pltpu.make_async_copy(nm_v, o_master.at[0], l_out.at[0]),
        pltpu.make_async_copy(n1_v, o_m1.at[0], l_out.at[1]),
        pltpu.make_async_copy(n2_v, o_m2.at[0], l_out.at[2]),
    ]
    for store in stores:
        store.start()

    next_part(0)
    z_part(0, 2)
    z_part(1, 1)
    new_hop(1)
    next_part(1)
    next_part(7)
    z_part(0, 3)
    z_part(1, 2)
    new_hop(2)
    next_part(2)
    next_part(6)
    z_part(0, 4)
    z_part(1, 3)
    new_hop(3)
    next_part(3)
    next_part(5)
    x_part(0)
    z_part(1, 4)
    new_hop(4)
    next_part(4)

    def next_copy(r):
        if r == 0:
            return remote(kvn.at[mates[0]], knr, s_k.at[0], r_k.at[0], mate_dev(mates[0]))
        return remote(kvs.at[r - 1], kns.at[r - 1], s_k.at[r], r_k.at[r], mate_dev(mates[r]))

    for r in (1, 2):
        kvs[r - 1] = kvn[mates[r]].astype(BF16)
        next_copy(r).start()
    next_copy(0).start()
    x_part(1)
    stores.append(pltpu.make_async_copy(oin_v, o_in, l_out.at[4]))
    stores[-1].start()
    with part_of("next_wait"):
        for r in range(3):
            next_copy(r).wait_recv()
    okv_v[...] = (kvn[q] + knr[...]) + (kns[0].astype(F32) + kns[1].astype(F32))
    stores.append(pltpu.make_async_copy(okv_v, o_kv.at[0], l_out.at[3]))
    stores[-1].start()

    wait_bytes(rmb.at[pl.ds(0, 3)], s_rm)
    for which in range(3):
        kv_copy(which).wait_send()
        next_copy(which).wait_send()
    for k in range(len(SETS)):
        wait_bytes(xa.at[0, pl.ds(0, 3), rows_of(0)], s_acts.at[k])
    for half in range(2):
        for r, mate in enumerate(mates):
            remote(msend.at[half], mrecv.at[half, r], s_m.at[half, r], r_m.at[half, r], mate_dev(mate)).wait_send()
        for slot in range(4):
            @pl.when(jnp.logical_not(stays(slot)))
            def _():
                x_copy(half, slot).wait_send()
    for way in range(2):
        for step in range(4):
            for part in range(2):
                if step < 3 or part == way:
                    gather_copy(wt, s_w, r_w, way, step, part).wait_send()
                    gather_copy(wn, s_n, r_n, way, step, part).wait_send()
                if step > 0 or part == way:
                    y_copy(way, step, part).wait_send()
                    z_copy(0, way, step, part).wait_send()
                    z_copy(1, way, step, part).wait_send()
    for store in stores:
        store.wait()


def write_out(*refs):
    sources, targets, held, got, done = refs[:5], refs[5:10], refs[10:15], refs[15], refs[16]
    loads = [pltpu.make_async_copy(sources[i], held[i], got.at[i]) for i in range(5)]
    stores = [pltpu.make_async_copy(held[i], targets[i], done.at[i]) for i in range(5)]
    for load in loads:
        load.start()
    for load, store in zip(loads, stores):
        load.wait()
        store.start()
    for store in stores:
        store.wait()


def per_device(acts, gain, kv_grad, master, moment_one, moment_two):
    anywhere = pl.BlockSpec(memory_space=pl.ANY)
    vmem = pltpu.VMEM
    dma = pltpu.SemaphoreType.DMA
    rows = jax.ShapeDtypeStruct((1, W, W), F32)
    scratch = [
        vmem((TOK, D), BF16),
        vmem((1, D), F32),
        vmem((W, W), F32), vmem((W, W), F32), vmem((W, W), F32),
        vmem((N, 4, TOK, W), BF16),
        vmem((4, TOK, W), BF16),
        vmem((4, W, TOK), BF16),
        vmem((4, 8, 128), F32),
        vmem((4, TOK, 128), F32),
        vmem((N, W, W), BF16),
        vmem((N, W, W), BF16),
        vmem((N, 4, TOK, W), BF16),
        vmem((N, 4, TOK, W), F32),
        vmem((2, 4, HALF, 128), F32),
        vmem((2, 8, 128), F32),
        vmem((2, 3, 8, 128), F32),
        vmem((2, 4, HALF, 128), F32),
        vmem((N, W, W), F32),
        vmem((2, 4, W, W), BF16), vmem((2, 4, W, W), BF16),
        vmem((2, 2, 4, 4, HALF, W), BF16), vmem((2, 2, 4, 4, HALF, W), BF16),
        vmem((2, 4, HALF, W), BF16), vmem((2, 4, HALF, W), BF16),
        vmem((4, TOK, W), F32), vmem((2, TOK, W), BF16),
        vmem((TOK, W), F32), vmem((2, TOK, W), BF16),
        vmem((W, W), F32), vmem((W, W), F32), vmem((W, W), F32),
        vmem((TOK, 2 * W), BF16),
        vmem((TOK, W), F32),
        dma((6,)), dma((N,)), dma((2 * N,)), dma((2 * N,)),
        dma((3,)), dma((3,)), dma, dma,
        dma((2, 3)), dma((2, 3)),
        dma((2, 4, 2)), dma((2, 4, 2)), dma((2, 4, 2)), dma((2, 4, 2)),
        dma((2, 4, 2)), dma((2, 4, 2)),
        dma((2, 2, 4, 2)), dma((2, 2, 4, 2)),
        dma((2, 4)), dma((2, 4)),
        dma((3,)), dma((3,)), dma((5,)),
    ]
    shapes = (
        rows, rows, rows,
        jax.ShapeDtypeStruct((TOK, 2 * W), BF16),
        jax.ShapeDtypeStruct((1, TOK, W), F32),
    )
    results = pl.pallas_call(
        kernel,
        out_shape=shapes,
        in_specs=[anywhere] * 6,
        out_specs=(anywhere,) * 5,
        scratch_shapes=scratch,
        compiler_params=pltpu.CompilerParams(
            collective_id=0, has_side_effects=True, vmem_limit_bytes=VMEM_BYTES
        ),
        cost_estimate=pl.CostEstimate(flops=1_700_000_000, bytes_accessed=6_000_000, transcendentals=200_000),
    )(acts, gain, kv_grad, master, moment_one, moment_two)
    return pl.pallas_call(
        write_out,
        out_shape=shapes,
        in_specs=[anywhere] * 5,
        out_specs=(anywhere,) * 5,
        scratch_shapes=[vmem(shape.shape, shape.dtype) for shape in shapes] + [dma((5,)), dma((5,))],
        compiler_params=pltpu.CompilerParams(vmem_limit_bytes=VMEM_BYTES),
        cost_estimate=pl.CostEstimate(flops=0, bytes_accessed=2_100_000, transcendentals=0),
    )(*results)


def solution(mesh):
    placed = (
        P("section", "dp", None),
        P("section", None),
        P("section", "dp", None),
        P("section", "dp", None),
        P("section", "dp", None),
        P("section", "dp", None),
    )
    return jax.shard_map(
        per_device,
        mesh=mesh,
        in_specs=placed,
        out_specs=(
            P("section", "dp", None),
            P("section", "dp", None),
            P("section", "dp", None),
            P("dp", "section"),
            P("section", "dp", None),
        ),
        check_vma=False,
    )
```

```python
import contextlib

import jax
import jax.numpy as jnp
from jax import lax
from jax.experimental import pallas as pl
from jax.experimental.pallas import tpu as pltpu
from jax.sharding import PartitionSpec as P

STEP = 20
NORM_EPS = 1e-05
ADAM_EPS = 1e-08
BETA_ONE = 0.9
BETA_TWO = 0.95
LEARN_RATE = 0.00015
DECAY_RATE = 0.1

F32 = jnp.float32
BF16 = jnp.bfloat16
MESH = pl.DeviceIdType.MESH
N = 8
D = 8192
TOK = 128
W = 256
VMEM_BYTES = 48 * 1024 * 1024
GROUPS = ((0, 64), (64, 32), (96, 32))
SETS = (
    (0, 0), (0, 7), (0, 1), (0, 2), (0, 6), (0, 5), (0, 3), (0, 4),
    (1, 4), (2, 4), (1, 3), (2, 3), (1, 5), (2, 5), (1, 2), (1, 6),
    (2, 6), (2, 2), (1, 7), (2, 7), (1, 1), (2, 1), (1, 0), (2, 0),
)
AHEAD = 5
HOLD = 24
STEPS = (
    ("relay",), ("old", 1, 0), ("old", 1, 1), ("prepare",), ("arrive", 0), ("arrive", 1), ("back", 0, 0),
    ("back", 0, 7), ("old", 2, 0), ("arrive", 2), ("back", 0, 1), ("old", 2, 1), ("arrive", 3), ("back", 0, 2),
    ("arrive", 4), ("back", 0, 6), ("old", 3, 0), ("arrive", 5), ("old", 3, 1), ("back", 0, 5), ("arrive", 6),
    ("back", 0, 3), ("old", 4, 0), ("arrive", 7), ("back", 0, 4), ("put", 0), ("arrive", 8), ("back", 1, 4),
    ("arrive", 9), ("grad", 4), ("ysum", 0, 0, 1), ("ysum", 1, 0, 1), ("back", 2, 4), ("arrive", 10), ("back", 1, 3),
    ("arrive", 11), ("grad", 3), ("back", 2, 3), ("arrive", 12), ("get", 0), ("zsum", 0, 0, 1, 0),
    ("zsum", 0, 1, 0, 0), ("zsum", 0, 0, 1, 1), ("zsum", 0, 1, 0, 1), ("back", 1, 5), ("arrive", 13), ("grad", 5),
    ("ysum", 0, 1, 0), ("ysum", 0, 1, 1), ("ysum", 1, 1, 0), ("back", 2, 5), ("arrive", 14), ("back", 1, 2),
    ("ysum", 1, 1, 1), ("arrive", 15), ("back", 1, 6), ("arrive", 16), ("grad", 6), ("zsum", 0, 1, 1, 0),
    ("back", 2, 6), ("arrive", 17), ("grad", 2), ("zsum", 0, 2, 0, 0), ("ysum", 0, 2, 0), ("back", 2, 2),
    ("arrive", 18), ("back", 1, 7), ("zsum", 0, 1, 1, 1), ("ysum", 0, 2, 1), ("arrive", 19), ("grad", 7),
    ("zsum", 0, 2, 0, 1), ("ysum", 1, 2, 0), ("back", 2, 7), ("arrive", 20), ("back", 1, 1), ("zsum", 0, 2, 1, 0),
    ("ysum", 1, 2, 1), ("arrive", 21), ("grad", 1), ("zsum", 0, 3, 0, 0), ("ysum", 0, 3, 0), ("back", 2, 1),
    ("arrive", 22), ("back", 1, 0), ("put", 1), ("zsum", 0, 2, 1, 1), ("ysum", 0, 3, 1), ("arrive", 23), ("grad", 0),
    ("back", 2, 0), ("put", 2), ("zsum", 0, 3, 0, 1), ("ysum", 1, 3, 0), ("zsum", 0, 3, 1, 0), ("ysum", 1, 3, 1),
    ("get", 1), ("zsum", 1, 0, 1, 0), ("zsum", 1, 1, 0, 0), ("get", 2), ("adam", 0), ("zsum", 2, 0, 1, 0),
    ("zsum", 2, 1, 0, 0), ("zsum", 0, 3, 1, 1), ("next", 0, 0), ("adam", 1), ("next", 1, 0), ("zsum", 1, 1, 1, 0),
    ("zsum", 1, 2, 0, 0), ("new", 0, 1, 0), ("zsum", 2, 1, 1, 0), ("new", 0, 1, 1), ("next", 0, 1), ("next", 0, 7),
    ("zsum", 2, 2, 0, 0), ("new", 1, 1, 0), ("zlast", 0), ("new", 1, 1, 1), ("next", 1, 1), ("next", 1, 7),
    ("zsum", 1, 2, 1, 0), ("new", 0, 2, 0), ("zsum", 1, 3, 0, 0), ("new", 0, 2, 1), ("next", 0, 2), ("next", 0, 6),
    ("zsum", 2, 2, 1, 0), ("new", 1, 2, 0), ("zsum", 2, 3, 0, 0), ("new", 1, 2, 1), ("next", 1, 2), ("next", 1, 6),
    ("zsum", 1, 3, 1, 0), ("new", 0, 3, 0), ("new", 0, 3, 1), ("next", 0, 3), ("next", 0, 5), ("zsum", 2, 3, 1, 0),
    ("new", 1, 3, 0), ("xlast", 0), ("new", 1, 3, 1), ("next", 1, 3), ("next", 1, 5), ("zlast", 1), ("new", 0, 4, 0),
    ("next", 0, 4), ("share", 0), ("zlast", 2), ("new", 1, 4, 0), ("next", 1, 4), ("share", 1), ("cross", 0),
    ("cross", 1), ("xlast", 1), ("finish", 0), ("xlast", 2), ("finish", 1),
)

def part_of(name):
    return contextlib.nullcontext()


def rows_of(group):
    return pl.ds(*GROUPS[group])


def part_rows(part):
    return pl.ds(part * 128, 128)


def wide(a):
    return jnp.concatenate([a, a], axis=-1)


def kernel(
    acts, gain, kv, master, mom1, mom2,
    o_master, o_m1, o_m2, o_in, o_kv,
    a_full, gain_v, mas_v, m1_v, m2_v,
    xa, kvb, kvt, rmb, invc, wt, wn, hid, sc, macc, msend, mrecv, mcol,
    gsum, ysend, yrecv, zsend, zrecv, xsend, xrecv, kvn, kvs, knc, knr, kns,
    l_in, l_acts, s_acts, s_kv, s_rm, s_m, s_w, s_n, s_y, s_z, s_x, s_k, s_kc,
    r_acts, r_kv, r_rm, r_m, r_w, r_n, r_y, r_z, r_x, r_k, r_kc,
):
    section = lax.axis_index("section")
    dp = lax.axis_index("dp")
    z = lax.div(section, 2)
    xh = lax.rem(section, 2)
    y = lax.div(dp, 4)
    q = lax.rem(dp, 4)
    xl = lax.div(q, 2)
    c = lax.rem(q, 2)
    mates = (xl * 2 + (1 - c), (1 - xl) * 2 + c, (1 - xl) * 2 + (1 - c))

    def ring(at, off):
        return lax.rem(at + off, N)

    def y_dev(off):
        return (section, ring(y, off) * 4 + q)

    def z_dev(off):
        return (ring(z, off) * 2 + xh, dp)

    def mate_dev(mate):
        return (section, y * 4 + mate)

    def remote(src, dst, send, recv, device):
        return pltpu.make_async_remote_copy(
            src_ref=src, dst_ref=dst, send_sem=send, recv_sem=recv, device_id=device, device_id_type=MESH
        )

    def wait_bytes(ref, sem):
        pltpu.make_async_copy(ref, ref, sem).wait()

    def columns(block):
        return pl.ds(pl.multiple_of(block * 1024 + q * W, W), W)

    barrier = pltpu.get_barrier_semaphore()
    for fh in range(2):
        for fl in range(2):
            for fc in range(2):
                if fh + fl + fc == 0:
                    continue
                other_h = 1 - xh if fh else xh
                other_l = 1 - xl if fl else xl
                other_c = 1 - c if fc else c
                device = (z * 2 + other_h, y * 4 + other_l * 2 + other_c)
                pl.semaphore_signal(barrier, inc=1, device_id=device, device_id_type=MESH)
    for device in (y_dev(1), y_dev(7), z_dev(1), z_dev(7)):
        pl.semaphore_signal(barrier, inc=1, device_id=device, device_id_type=MESH)

    loads = [
        pltpu.make_async_copy(kv.at[0], kvb.at[q], l_in.at[0]),
        pltpu.make_async_copy(master.at[0], mas_v, l_in.at[1]),
        pltpu.make_async_copy(acts.at[0], a_full, l_in.at[2]),
        pltpu.make_async_copy(gain, gain_v, l_in.at[3]),
        pltpu.make_async_copy(mom1.at[0], m1_v, l_in.at[4]),
        pltpu.make_async_copy(mom2.at[0], m2_v, l_in.at[5]),
    ]
    for load in loads:
        load.start()
    for off in range(N):
        block = ring(y, off)
        pltpu.make_async_copy(acts.at[0, :, columns(block)], xa.at[block, q], l_acts).start()

    with part_of("barrier"):
        pl.semaphore_wait(barrier, 11)

    def send_acts(k):
        group, off = SETS[k]
        rows = rows_of(group)
        block = ring(y, off)
        for mate in mates:
            source = acts.at[0, rows, pl.ds(pl.multiple_of(block * 1024 + mate * W, W), W)]
            remote(source, xa.at[block, q, rows], s_acts, r_acts.at[k], mate_dev(mate)).start()

    def kv_copy(which):
        slot, mate = ((q, mates[0]), (q, mates[1]), (mates[1], mates[0]))[which]
        return remote(kvb.at[slot], kvb.at[slot], s_kv, r_kv.at[which], mate_dev(mate))

    def gather_send(buffer, send, recv, hop, k):
        for way in range(2):
            block = ring(y, N - hop if way == 0 else hop)
            rows = buffer.at[block, part_rows(k if way == 0 else 1 - k)]
            remote(rows, rows, send, recv.at[hop, k], y_dev(1 if way == 0 else 7)).start()

    def gather_step(buffer, send, recv, hop, k):
        wait_bytes(buffer.at[0], recv.at[hop - 1, k])
        if hop < 3 or (hop == 3 and k == 0):
            gather_send(buffer, send, recv, hop, k)

    loads[0].wait()
    kv_copy(1).start()
    kv_copy(0).start()
    send_acts(0)
    send_acts(1)
    with part_of("wt"):
        loads[1].wait()
        wt[y] = jnp.transpose(mas_v[...]).astype(BF16)
    for k in range(2):
        gather_send(wt, s_w, r_w, 0, k)

    with part_of("squares"):
        loads[2].wait()

        def add_squares(step, total):
            part = a_full[:, pl.ds(pl.multiple_of(step * 512, 512), 512)].astype(F32)
            part = part * part
            return total + ((part[:, :128] + part[:, 128:256]) + (part[:, 256:384] + part[:, 384:]))

        squares = lax.fori_loop(0, 16, add_squares, jnp.zeros((TOK, 128), F32))
        mean_row = jnp.sum(jnp.transpose(squares), axis=0, keepdims=True) / D
        rmb[q] = jnp.broadcast_to(jnp.sqrt(mean_row + NORM_EPS), (8, 128))
    for mate in mates:
        remote(rmb.at[q], rmb.at[q], s_rm, r_rm, mate_dev(mate)).start()
    for k in range(2, min(AHEAD, HOLD)):
        send_acts(k)
    sent = [min(AHEAD, HOLD), False, -1]
    macc[...] = jnp.zeros_like(macc)
    loads[3].wait()
    wait_bytes(xa.at[pl.ds(0, 2)], l_acts)

    def relay():
        kv_copy(1).wait_recv()
        kv_copy(2).start()

    def prepare():
        kv_copy(0).wait_recv()
        kv_copy(2).wait_recv()
        wait_bytes(rmb.at[pl.ds(0, 3)], r_rm)

        def one(slot, carry):
            root = jnp.transpose(jnp.broadcast_to(rmb[slot][0:1, :], (128, 128)))
            invc[slot] = 1.0 / root
            kvt[slot] = jnp.transpose(kvb[slot].astype(F32)).astype(BF16)
            return carry

        lax.fori_loop(0, 4, one, 0)

    def old(hop, k):
        gather_step(wt, s_w, r_w, hop, k)

    def new(half, hop, k):
        gather_step(wn.at[:, half], s_n, r_n.at[half], hop, k)

    def feed(k):
        for later in range(sent[0], min(k + 1 + AHEAD, len(SETS) if sent[1] else HOLD)):
            send_acts(later)
            sent[0] = later + 1
        sent[2] = k

    def arrive(k):
        group, off = SETS[k]
        rows = rows_of(group)
        wait_bytes(xa.at[0, pl.ds(0, 3), rows], r_acts.at[k])
        feed(k)
        block = ring(y, off)
        gain_row = gain_v[:, columns(block)]

        def one(slot, carry):
            unit = xa[block, slot, rows, :].astype(F32) * wide(invc[slot, rows, :])
            hid[block, slot, rows, :] = (unit * gain_row).astype(BF16)
            return carry

        lax.fori_loop(0, 4, one, 0)

    def back(group, off):
        rows = rows_of(group)
        count = GROUPS[group][1]
        block = ring(y, off)
        gain_row = gain_v[:, columns(block)]
        product = jnp.dot(kvb[:, rows, :].reshape(4 * count, W), wt[block], preferred_element_type=F32)
        sc[block, :, rows, :] = product.reshape(4, count, W)

        def one(slot, carry):
            unit = xa[block, slot, rows, :].astype(F32) * wide(invc[slot, rows, :])
            scaled = sc[block, slot, rows, :] * gain_row
            sc[block, slot, rows, :] = scaled
            both = scaled * unit
            macc[slot, rows, :] += both[:, :128] + both[:, 128:]
            return carry

        lax.fori_loop(0, 4, one, 0)

    def grad(off):
        block = ring(y, off)
        total = None
        for slot in range(4):
            product = jnp.dot(kvt[slot], hid[block, slot], preferred_element_type=F32).astype(BF16).astype(F32)
            total = product if total is None else total + product
        gsum[block] = total

    def put(group):
        rows = rows_of(group)
        slots = 128 // GROUPS[group][1]
        msend[group] = jnp.zeros((8, 128), F32)
        for row in range(4 // slots):
            both = macc[pl.ds(row * slots, slots), rows].reshape(128, 128)
            msend[group, row : row + 1, :] = jnp.sum(jnp.transpose(both), axis=0, keepdims=True)
        for r, mate in enumerate(mates):
            remote(msend.at[group], mrecv.at[group, r], s_m, r_m.at[group], mate_dev(mate)).start()
        sent[1] = True
        feed(sent[2])

    def get(group):
        wait_bytes(mrecv.at[group], r_m.at[group])
        total = ((msend[group] + mrecv[group, 0]) + (mrecv[group, 1] + mrecv[group, 2])) / D
        slots = 128 // GROUPS[group][1]
        for row in range(4 // slots):
            column = jnp.transpose(jnp.broadcast_to(total[row : row + 1, :], (128, 128)))
            mcol[pl.ds(row * slots, slots), rows_of(group)] = column.reshape(slots, GROUPS[group][1], 128)

    def branch(group, block, slot):
        rows = rows_of(group)
        inv = wide(invc[slot, rows, :])
        unit = xa[block, slot, rows, :].astype(F32) * inv
        return ((sc[block, slot, rows, :] - unit * wide(mcol[slot, rows])) * inv).astype(BF16)

    def ysum(half, step, k):
        adds = step > 1 or (step == 1 and k == 1)
        if adds:
            wait_bytes(yrecv.at[0, 0, part_rows(0)], r_y.at[half, step - 1, k])
        for way in range(2):
            part = way if k == 1 else 1 - way
            rows = pl.ds(half * 128 + part * 64, 64)
            total = gsum[ring(y, 4 - step if way == 0 else 4 + step), rows]
            if adds:
                total = total + yrecv[way, step - 1, rows].astype(F32)
            ysend[way, step, rows] = total.astype(BF16)
            remote(
                ysend.at[way, step, rows], yrecv.at[way, step, rows], s_y, r_y.at[half, step, k],
                y_dev(1 if way == 0 else 7),
            ).start()

    def z_sem(group, step, k, j):
        return r_z.at[step * 4 + k * 2 + j if group == 0 else 8 + group * 8 + step * 2 + k]

    z_bytes = zrecv.at[0, 0, pl.ds(0, 2), rows_of(0)]

    def zsum(group, step, k, j):
        rows = rows_of(group)
        slots = 1 if group == 0 else 2
        adds = step > 1 or (step == 1 and k == 1)
        if adds:
            wait_bytes(z_bytes, z_sem(group, step - 1, k, j))
        for way in range(2):
            first = 2 * (way if k == 1 else 1 - way) + j
            for slot in range(first, first + slots):
                own = branch(group, ring(z, 4 - step if way == 0 else 4 + step), slot)
                if adds:
                    own = (own.astype(F32) + zrecv[way, step - 1, slot, rows].astype(F32)).astype(BF16)
                zsend[way, step, slot, rows] = own
            part = pl.ds(first, slots)
            remote(
                zsend.at[way, step, part, rows], zrecv.at[way, step, part, rows], s_z, z_sem(group, step, k, j),
                z_dev(1 if way == 0 else 7),
            ).start()

    x_section = z * 2 + xl
    x_source = xh * 2 + c

    def zlast(group):
        rows = rows_of(group)
        for k in range(2):
            for j in range(2 if group == 0 else 1):
                wait_bytes(z_bytes, z_sem(group, 3, k, j))

        def one(slot, carry):
            total = branch(group, z, slot).astype(F32)
            total = total + (zrecv[0, 3, slot, rows].astype(F32) + zrecv[1, 3, slot, rows].astype(F32))
            xsend[slot, rows] = total.astype(BF16)
            return carry

        lax.fori_loop(0, 4, one, 0)
        for slot in range(4):
            stays = jnp.logical_and(xh == xl, q == slot)

            @pl.when(stays)
            def _():
                pltpu.make_async_copy(xsend.at[slot, rows], xrecv.at[x_source, rows], r_x.at[group]).start()

            @pl.when(jnp.logical_not(stays))
            def _():
                remote(
                    xsend.at[slot, rows], xrecv.at[x_source, rows], s_x, r_x.at[group], (x_section, y * 4 + slot)
                ).start()

    ended = {"adam": 0}

    def xlast(group):
        rows = rows_of(group)
        wait_bytes(xrecv.at[:, rows], r_x.at[group])
        for col in range(2):
            total = xrecv[col, rows].astype(F32) + xrecv[2 + col, rows].astype(F32)
            o_in[rows, col * W : (col + 1) * W] = total.astype(BF16)

    def adam(half):
        for k in range(2):
            wait_bytes(yrecv.at[0, 0, part_rows(0)], r_y.at[half, 3, k])
        ended["adam"] += 1
        if ended["adam"] == 1:
            for load in loads[4:]:
                load.wait()
        rows = part_rows(half)
        cols = slice(half * 128, half * 128 + 128)
        gradient = jnp.transpose(gsum[y, rows] + (yrecv[0, 3, rows].astype(F32) + yrecv[1, 3, rows].astype(F32)))
        was = mas_v[:, cols]
        first_new = BETA_ONE * m1_v[:, cols] + (1.0 - BETA_ONE) * gradient
        second_new = BETA_TWO * m2_v[:, cols] + (1.0 - BETA_TWO) * gradient * gradient
        direction = (
            first_new / (1.0 - BETA_ONE**STEP) / (jnp.sqrt(second_new / (1.0 - BETA_TWO**STEP)) + ADAM_EPS)
        )
        updated = was - LEARN_RATE * (direction + DECAY_RATE * was)
        wn[y, half] = updated.astype(BF16)
        for k in range(2):
            gather_send(wn.at[:, half], s_n, r_n.at[half], 0, k)
        o_master[0, :, cols] = updated
        o_m1[0, :, cols] = first_new
        o_m2[0, :, cols] = second_new

    def next(half, off):
        block = ring(y, off)
        part = jnp.dot(hid[block].reshape(4 * TOK, W), wn[block, half], preferred_element_type=F32)
        part = part.reshape(4, TOK, 128)
        kvn[half] = part if off == 0 else kvn[half] + part

    def share(half):
        remote(kvn.at[half, mates[2]], knc.at[half], s_kc, r_kc.at[half], mate_dev(mates[0])).start()
        remote(kvn.at[half, mates[0]], knr.at[half], s_kc, r_k.at[half], mate_dev(mates[0])).start()

    def cross(half):
        wait_bytes(knc.at[half], r_kc.at[half])
        kvs[half] = (kvn[half, mates[1]] + knc[half]).astype(BF16)
        remote(kvs.at[half], kns.at[half], s_k, r_k.at[half], mate_dev(mates[1])).start()

    def finish(half):
        wait_bytes(xa.at[0, pl.ds(0, 3), rows_of(0)], r_k.at[half])
        total = (kvn[half, q] + knr[half]) + kns[half].astype(F32)
        o_kv[0, :, half * 128 : half * 128 + 128] = total

    takes = {
        "relay": relay, "prepare": prepare, "old": old, "new": new, "arrive": arrive, "back": back, "grad": grad,
        "put": put, "get": get, "ysum": ysum, "zsum": zsum, "zlast": zlast, "xlast": xlast, "adam": adam,
        "next": next, "share": share, "cross": cross, "finish": finish,
    }
    for name, *where in STEPS:
        with part_of(name + "_".join(str(n) for n in where)):
            takes[name](*where)

    with part_of("sent"):
        wait_bytes(xa.at[pl.ds(0, 6)], s_acts)
        wait_bytes(kvb.at[pl.ds(0, 3)], s_kv)
        wait_bytes(rmb.at[pl.ds(0, 3)], s_rm)
        wait_bytes(mrecv, s_m)
        wait_bytes(wt.at[pl.ds(0, 7)], s_w)
        wait_bytes(wn.at[pl.ds(0, 7)], s_n)
        wait_bytes(wt.at[pl.ds(0, 7)], s_y)
        wait_bytes(hid.at[pl.ds(0, 7)], s_z)
        wait_bytes(kvn.at[0], s_kc)
        wait_bytes(kvs, s_k)

        @pl.when(xh == xl)
        def _():
            wait_bytes(xsend.at[pl.ds(0, 3)], s_x)

        @pl.when(xh != xl)
        def _():
            wait_bytes(xsend, s_x)


def write_out(*refs):
    sources, targets, done = refs[:5], refs[5:10], refs[10]
    copies = [pltpu.make_async_copy(sources[i], targets[i], done.at[i]) for i in range(5)]
    for copy in copies:
        copy.start()
    for copy in copies:
        copy.wait()


def per_device(acts, gain, kv_grad, master, moment_one, moment_two):
    anywhere = pl.BlockSpec(memory_space=pl.ANY)
    vmem = pltpu.VMEM
    dma = pltpu.SemaphoreType.DMA
    rows = jax.ShapeDtypeStruct((1, W, W), F32)
    scratch = [
        vmem((TOK, D), BF16),
        vmem((1, D), F32),
        vmem((W, W), F32), vmem((W, W), F32), vmem((W, W), F32),
        vmem((N, 4, TOK, W), BF16),
        vmem((4, TOK, W), BF16),
        vmem((4, W, TOK), BF16),
        vmem((4, 8, 128), F32),
        vmem((4, TOK, 128), F32),
        vmem((N, W, W), BF16), vmem((N, 2, W, 128), BF16),
        vmem((N, 4, TOK, W), BF16),
        vmem((N, 4, TOK, W), F32),
        vmem((4, TOK, 128), F32),
        vmem((len(GROUPS), 8, 128), F32),
        vmem((len(GROUPS), 3, 8, 128), F32),
        vmem((4, TOK, 128), F32),
        vmem((N, W, W), F32),
        vmem((2, 4, W, W), BF16), vmem((2, 4, W, W), BF16),
        vmem((2, 4, 4, TOK, W), BF16), vmem((2, 4, 4, TOK, W), BF16),
        vmem((4, TOK, W), BF16), vmem((4, TOK, W), BF16),
        vmem((2, 4, TOK, 128), F32), vmem((2, TOK, 128), BF16),
        vmem((2, TOK, 128), F32), vmem((2, TOK, 128), F32), vmem((2, TOK, 128), BF16),
        dma((6,)), dma,
        dma, dma, dma, dma, dma, dma, dma, dma, dma, dma, dma,
        dma((len(SETS),)), dma((3,)), dma, dma((len(GROUPS),)),
        dma((4, 2)), dma((2, 4, 2)), dma((2, 4, 2)), dma((32,)),
        dma((len(GROUPS),)), dma((2,)), dma((2,)),
    ]
    shapes = (
        rows, rows, rows,
        jax.ShapeDtypeStruct((TOK, 2 * W), BF16),
        jax.ShapeDtypeStruct((1, TOK, W), F32),
    )
    given = [
        pltpu.with_memory_space_constraint(a, pltpu.HBM)
        for a in (acts, gain, kv_grad, master, moment_one, moment_two)
    ]
    results = pl.pallas_call(
        kernel,
        out_shape=tuple(vmem(shape.shape, shape.dtype) for shape in shapes),
        in_specs=[pl.BlockSpec(memory_space=pltpu.HBM)] * 6,
        out_specs=(pl.BlockSpec(memory_space=pltpu.VMEM),) * 5,
        scratch_shapes=scratch,
        compiler_params=pltpu.CompilerParams(
            collective_id=0, has_side_effects=True, vmem_limit_bytes=VMEM_BYTES
        ),
        cost_estimate=pl.CostEstimate(flops=1_700_000_000, bytes_accessed=6_000_000, transcendentals=200_000),
    )(*given)
    return pl.pallas_call(
        write_out,
        out_shape=shapes,
        in_specs=[pl.BlockSpec(memory_space=pltpu.VMEM)] * 5,
        out_specs=(anywhere,) * 5,
        scratch_shapes=[dma((5,))],
        cost_estimate=pl.CostEstimate(flops=0, bytes_accessed=2_100_000, transcendentals=0),
    )(*[pltpu.with_memory_space_constraint(a, pltpu.VMEM) for a in results])


def solution(mesh):
    placed = (
        P("section", "dp", None),
        P("section", None),
        P("section", "dp", None),
        P("section", "dp", None),
        P("section", "dp", None),
        P("section", "dp", None),
    )
    return jax.shard_map(
        per_device,
        mesh=mesh,
        in_specs=placed,
        out_specs=(
            P("section", "dp", None),
            P("section", "dp", None),
            P("section", "dp", None),
            P("dp", "section"),
            P("section", "dp", None),
        ),
        check_vma=False,
    )
```

```python
import contextlib

import jax
import jax.numpy as jnp
from jax import lax
from jax.experimental import pallas as pl
from jax.experimental.pallas import tpu as pltpu
from jax.sharding import PartitionSpec as P

STEP = 20
NORM_EPS = 1e-05
ADAM_EPS = 1e-08
BETA_ONE = 0.9
BETA_TWO = 0.95
LEARN_RATE = 0.00015
DECAY_RATE = 0.1

F32 = jnp.float32
BF16 = jnp.bfloat16
MESH = pl.DeviceIdType.MESH
N = 8
D = 8192
TOK = 128
W = 256
VMEM_BYTES = 48 * 1024 * 1024
GROUPS = ((0, 64), (64, 32), (96, 32))
SETS = (
    (0, 0), (0, 4), (0, 7), (0, 1), (0, 5), (0, 3), (0, 2), (0, 6),
    (1, 4), (2, 4), (1, 3), (2, 3), (1, 5), (2, 5), (1, 6), (2, 6),
    (1, 2), (2, 2), (1, 7), (2, 7), (1, 1), (2, 1), (1, 0), (2, 0),
)
AHEAD = 7
HOLD = 24
STEPS = (
    ("relay",), ("old", 1, 0), ("old", 1, 1), ("prepare",), ("project", 0), ("project", 1), ("project", 7),
    ("arrive", 0), ("back", 0, 0), ("arrive", 1), ("arrive", 2), ("old", 2, 0), ("back", 0, 7), ("arrive", 3),
    ("back", 0, 1), ("old", 2, 1), ("project", 2), ("project", 6), ("arrive", 4), ("arrive", 5), ("old", 3, 0),
    ("arrive", 6), ("back", 0, 2), ("old", 3, 1), ("project", 3), ("back", 0, 3), ("project", 5), ("back", 0, 5),
    ("arrive", 7), ("back", 0, 6), ("old", 4, 0), ("project", 4), ("back", 0, 4), ("put", 0), ("arrive", 10),
    ("arrive", 8), ("arrive", 9), ("grad", 4), ("ysum", 0, 0, 1), ("ysum", 1, 0, 1), ("arrive", 11), ("grad", 3),
    ("arrive", 12), ("arrive", 13), ("grad", 5), ("ysum", 0, 1, 0), ("ysum", 1, 1, 0), ("arrive", 14), ("get", 0),
    ("zsum", 0, 0, 1, 0), ("zsum", 0, 0, 1, 1), ("zsum", 0, 1, 0, 0), ("zsum", 0, 1, 0, 1), ("arrive", 15),
    ("grad", 6), ("ysum", 0, 1, 1), ("arrive", 16), ("ysum", 1, 1, 1), ("arrive", 17), ("grad", 2), ("arrive", 18),
    ("ysum", 0, 2, 0), ("zsum", 0, 1, 1, 0), ("arrive", 19), ("grad", 7), ("ysum", 1, 2, 0), ("zsum", 0, 1, 1, 1),
    ("arrive", 20), ("ysum", 0, 2, 1), ("zsum", 0, 2, 0, 0), ("arrive", 21), ("grad", 1), ("ysum", 1, 2, 1),
    ("zsum", 0, 2, 0, 1), ("arrive", 22), ("put", 1), ("ysum", 0, 3, 0), ("arrive", 23), ("put", 2), ("grad", 0),
    ("zsum", 0, 2, 1, 0), ("ysum", 1, 3, 0), ("zsum", 0, 2, 1, 1), ("ysum", 0, 3, 1), ("get", 1),
    ("zsum", 1, 0, 1, 0), ("zsum", 1, 1, 0, 0), ("zsum", 0, 3, 0, 0), ("ysum", 1, 3, 1), ("get", 2),
    ("zsum", 2, 0, 1, 0), ("zsum", 2, 1, 0, 0), ("zsum", 0, 3, 0, 1), ("zsum", 0, 3, 1, 0), ("adam", 0),
    ("next", 0, 0), ("zsum", 1, 1, 1, 0), ("adam", 1), ("next", 1, 0), ("zsum", 1, 2, 0, 0), ("zsum", 0, 3, 1, 1),
    ("zsum", 2, 1, 1, 0), ("new", 0, 1, 0), ("zsum", 2, 2, 0, 0), ("new", 0, 1, 1), ("next", 0, 1), ("next", 0, 7),
    ("new", 1, 1, 0), ("new", 1, 1, 1), ("next", 1, 1), ("next", 1, 7), ("zsum", 1, 2, 1, 0), ("new", 0, 2, 0),
    ("zlast", 0), ("zsum", 1, 3, 0, 0), ("new", 0, 2, 1), ("next", 0, 2), ("next", 0, 6), ("zsum", 2, 2, 1, 0),
    ("new", 1, 2, 0), ("zsum", 2, 3, 0, 0), ("new", 1, 2, 1), ("next", 1, 2), ("next", 1, 6), ("zsum", 1, 3, 1, 0),
    ("new", 0, 3, 0), ("new", 0, 3, 1), ("next", 0, 3), ("next", 0, 5), ("zsum", 2, 3, 1, 0), ("new", 1, 3, 0),
    ("new", 1, 3, 1), ("next", 1, 3), ("next", 1, 5), ("xlast", 0), ("zlast", 1), ("new", 0, 4, 0), ("next", 0, 4),
    ("share", 0), ("cross", 0), ("new", 1, 4, 0), ("next", 1, 4), ("share", 1), ("zlast", 2), ("cross", 1),
    ("xlast", 1), ("finish", 0), ("xlast", 2), ("finish", 1),
)

def part_of(name):
    return contextlib.nullcontext()


def rows_of(group):
    return pl.ds(*GROUPS[group])


def part_rows(part):
    return pl.ds(part * 128, 128)


def wide(a):
    return jnp.concatenate([a, a], axis=-1)


def kernel(
    acts, gain, kv, master, mom1, mom2,
    o_master, o_m1, o_m2, o_in, o_kv,
    a_full, gain_v, mas_v, m1_v, m2_v,
    xa, kvb, kvt, rmb, invc, wt, wn, hid, sc, macc, msend, mrecv, mcol,
    gsum, ysend, yrecv, zsend, zrecv, xsend, xrecv, kvn, kvs, knc, knr, kns,
    l_in, l_acts, s_acts, s_kv, s_rm, s_m, s_w, s_n, s_y, s_z, s_x, s_k, s_kc,
    r_acts, r_kv, r_rm, r_m, r_w, r_n, r_y, r_z, r_x, r_k, r_kc,
):
    section = lax.axis_index("section")
    dp = lax.axis_index("dp")
    z = lax.div(section, 2)
    xh = lax.rem(section, 2)
    y = lax.div(dp, 4)
    q = lax.rem(dp, 4)
    xl = lax.div(q, 2)
    c = lax.rem(q, 2)
    mates = (xl * 2 + (1 - c), (1 - xl) * 2 + c, (1 - xl) * 2 + (1 - c))

    def ring(at, off):
        return lax.rem(at + off, N)

    def y_dev(off):
        return (section, ring(y, off) * 4 + q)

    def z_dev(off):
        return (ring(z, off) * 2 + xh, dp)

    def mate_dev(mate):
        return (section, y * 4 + mate)

    def remote(src, dst, send, recv, device):
        return pltpu.make_async_remote_copy(
            src_ref=src, dst_ref=dst, send_sem=send, recv_sem=recv, device_id=device, device_id_type=MESH
        )

    def wait_bytes(ref, sem):
        pltpu.make_async_copy(ref, ref, sem).wait()

    def columns(block):
        return pl.ds(pl.multiple_of(block * 1024 + q * W, W), W)

    barrier = pltpu.get_barrier_semaphore()
    for fh in range(2):
        for fl in range(2):
            for fc in range(2):
                if fh + fl + fc == 0:
                    continue
                other_h = 1 - xh if fh else xh
                other_l = 1 - xl if fl else xl
                other_c = 1 - c if fc else c
                device = (z * 2 + other_h, y * 4 + other_l * 2 + other_c)
                pl.semaphore_signal(barrier, inc=1, device_id=device, device_id_type=MESH)
    for device in (y_dev(1), y_dev(7), z_dev(1), z_dev(7)):
        pl.semaphore_signal(barrier, inc=1, device_id=device, device_id_type=MESH)

    loads = [
        pltpu.make_async_copy(kv.at[0], kvb.at[q], l_in.at[0]),
        pltpu.make_async_copy(master.at[0], mas_v, l_in.at[1]),
        pltpu.make_async_copy(acts.at[0], a_full, l_in.at[2]),
        pltpu.make_async_copy(gain, gain_v, l_in.at[3]),
        pltpu.make_async_copy(mom1.at[0], m1_v, l_in.at[4]),
        pltpu.make_async_copy(mom2.at[0], m2_v, l_in.at[5]),
    ]
    for load in loads:
        load.start()
    for off in range(N):
        block = ring(y, off)
        pltpu.make_async_copy(acts.at[0, :, columns(block)], xa.at[block, q], l_acts).start()

    with part_of("barrier"):
        pl.semaphore_wait(barrier, 11)

    def send_acts(k):
        group, off = SETS[k]
        rows = rows_of(group)
        block = ring(y, off)
        for mate in mates:
            source = acts.at[0, rows, pl.ds(pl.multiple_of(block * 1024 + mate * W, W), W)]
            remote(source, xa.at[block, q, rows], s_acts, r_acts.at[k], mate_dev(mate)).start()

    def kv_copy(which):
        slot, mate = ((q, mates[0]), (q, mates[1]), (mates[1], mates[0]))[which]
        return remote(kvb.at[slot], kvb.at[slot], s_kv, r_kv.at[which], mate_dev(mate))

    def gather_send(buffer, send, recv, hop, k):
        for way in range(2):
            block = ring(y, N - hop if way == 0 else hop)
            rows = buffer.at[block, part_rows(k if way == 0 else 1 - k)]
            remote(rows, rows, send, recv.at[hop, k], y_dev(1 if way == 0 else 7)).start()

    def gather_step(buffer, send, recv, hop, k):
        wait_bytes(buffer.at[0], recv.at[hop - 1, k])
        if hop < 3 or (hop == 3 and k == 0):
            gather_send(buffer, send, recv, hop, k)

    loads[0].wait()
    kv_copy(1).start()
    kv_copy(0).start()
    send_acts(0)
    send_acts(1)
    with part_of("wt"):
        loads[1].wait()
        wt[y] = jnp.transpose(mas_v[...]).astype(BF16)
    for k in range(2):
        gather_send(wt, s_w, r_w, 0, k)

    with part_of("squares"):
        loads[2].wait()

        def add_squares(step, total):
            part = a_full[:, pl.ds(pl.multiple_of(step * 512, 512), 512)].astype(F32)
            part = part * part
            return total + ((part[:, :128] + part[:, 128:256]) + (part[:, 256:384] + part[:, 384:]))

        squares = lax.fori_loop(0, 16, add_squares, jnp.zeros((TOK, 128), F32))
        mean_row = jnp.sum(jnp.transpose(squares), axis=0, keepdims=True) / D
        rmb[q] = jnp.broadcast_to(jnp.sqrt(mean_row + NORM_EPS), (8, 128))
    for mate in mates:
        remote(rmb.at[q], rmb.at[q], s_rm, r_rm, mate_dev(mate)).start()
    for k in range(2, min(AHEAD, HOLD)):
        send_acts(k)
    sent = [min(AHEAD, HOLD), False, -1]
    macc[...] = jnp.zeros_like(macc)
    loads[3].wait()
    wait_bytes(xa.at[pl.ds(0, 2)], l_acts)

    def relay():
        kv_copy(1).wait_recv()
        kv_copy(2).start()

    def prepare():
        kv_copy(0).wait_recv()
        kv_copy(2).wait_recv()
        wait_bytes(rmb.at[pl.ds(0, 3)], r_rm)

        def one(slot, carry):
            root = jnp.transpose(jnp.broadcast_to(rmb[slot][0:1, :], (128, 128)))
            invc[slot] = 1.0 / root
            return carry

        lax.fori_loop(0, 4, one, 0)
        for slot in range(4):
            kvt[:, slot * TOK : (slot + 1) * TOK] = jnp.transpose(kvb[slot].astype(F32)).astype(BF16)

    def old(hop, k):
        gather_step(wt, s_w, r_w, hop, k)

    def new(half, hop, k):
        gather_step(wn.at[:, half], s_n, r_n.at[half], hop, k)

    def feed(k):
        for later in range(sent[0], min(k + 1 + AHEAD, len(SETS) if sent[1] else HOLD)):
            send_acts(later)
            sent[0] = later + 1
        sent[2] = k

    def project(off):
        block = ring(y, off)
        product = jnp.dot(kvb[...].reshape(4 * TOK, W), wt[block], preferred_element_type=F32)
        sc[block] = (product * gain_v[:, columns(block)]).reshape(4, TOK, W)
        projected.add(off)

    projected = set()
    hidden_only = set()

    def features(group, off, hides, means):
        rows = rows_of(group)
        block = ring(y, off)
        gain_row = gain_v[:, columns(block)]

        def one(slot, carry):
            unit = xa[block, slot, rows, :].astype(F32) * wide(invc[slot, rows, :])
            if hides:
                hid[block, slot, rows, :] = (unit * gain_row).astype(BF16)
            if means:
                both = sc[block, slot, rows, :] * unit
                macc[slot, rows, :] += both[:, :128] + both[:, 128:]
            return carry

        lax.fori_loop(0, 4, one, 0)

    def arrive(k):
        group, off = SETS[k]
        wait_bytes(xa.at[0, pl.ds(0, 3), rows_of(group)], r_acts.at[k])
        feed(k)
        features(group, off, True, off in projected)
        if off not in projected:
            hidden_only.add((group, off))

    def back(group, off):
        if (group, off) in hidden_only:
            features(group, off, False, True)

    def grad(off):
        block = ring(y, off)
        gsum[block] = jnp.dot(kvt[...], hid[block].reshape(4 * TOK, W), preferred_element_type=F32)

    def put(group):
        rows = rows_of(group)
        slots = 128 // GROUPS[group][1]
        msend[group] = jnp.zeros((8, 128), F32)
        for row in range(4 // slots):
            both = macc[pl.ds(row * slots, slots), rows].reshape(128, 128)
            msend[group, row : row + 1, :] = jnp.sum(jnp.transpose(both), axis=0, keepdims=True)
        for r, mate in enumerate(mates):
            remote(msend.at[group], mrecv.at[group, r], s_m, r_m.at[group], mate_dev(mate)).start()
        sent[1] = True
        feed(sent[2])

    def get(group):
        wait_bytes(mrecv.at[group], r_m.at[group])
        total = ((msend[group] + mrecv[group, 0]) + (mrecv[group, 1] + mrecv[group, 2])) / D
        slots = 128 // GROUPS[group][1]
        for row in range(4 // slots):
            column = jnp.transpose(jnp.broadcast_to(total[row : row + 1, :], (128, 128)))
            mcol[pl.ds(row * slots, slots), rows_of(group)] = column.reshape(slots, GROUPS[group][1], 128)

    def branch(group, block, slot):
        rows = rows_of(group)
        inv = wide(invc[slot, rows, :])
        unit = xa[block, slot, rows, :].astype(F32) * inv
        return ((sc[block, slot, rows, :] - unit * wide(mcol[slot, rows])) * inv).astype(BF16)

    def ysum(half, step, k):
        adds = step > 1 or (step == 1 and k == 1)
        if adds:
            wait_bytes(yrecv.at[0, 0, part_rows(0)], r_y.at[half, step - 1, k])
        for way in range(2):
            part = way if k == 1 else 1 - way
            rows = pl.ds(half * 128 + part * 64, 64)
            total = gsum[ring(y, 4 - step if way == 0 else 4 + step), rows]
            if adds:
                total = total + yrecv[way, step - 1, rows].astype(F32)
            ysend[way, step, rows] = total.astype(BF16)
            remote(
                ysend.at[way, step, rows], yrecv.at[way, step, rows], s_y, r_y.at[half, step, k],
                y_dev(1 if way == 0 else 7),
            ).start()

    def z_sem(group, step, k, j):
        return r_z.at[step * 4 + k * 2 + j if group == 0 else 8 + group * 8 + step * 2 + k]

    z_bytes = zrecv.at[0, 0, pl.ds(0, 2), rows_of(0)]

    def zsum(group, step, k, j):
        rows = rows_of(group)
        slots = 1 if group == 0 else 2
        adds = step > 1 or (step == 1 and k == 1)
        if adds:
            wait_bytes(z_bytes, z_sem(group, step - 1, k, j))
        for way in range(2):
            first = 2 * (way if k == 1 else 1 - way) + j
            for slot in range(first, first + slots):
                own = branch(group, ring(z, 4 - step if way == 0 else 4 + step), slot)
                if adds:
                    own = (own.astype(F32) + zrecv[way, step - 1, slot, rows].astype(F32)).astype(BF16)
                zsend[way, step, slot, rows] = own
            part = pl.ds(first, slots)
            remote(
                zsend.at[way, step, part, rows], zrecv.at[way, step, part, rows], s_z, z_sem(group, step, k, j),
                z_dev(1 if way == 0 else 7),
            ).start()

    x_section = z * 2 + xl
    x_source = xh * 2 + c

    def zlast(group):
        rows = rows_of(group)
        for k in range(2):
            for j in range(2 if group == 0 else 1):
                wait_bytes(z_bytes, z_sem(group, 3, k, j))

        def one(slot, carry):
            total = branch(group, z, slot).astype(F32)
            total = total + (zrecv[0, 3, slot, rows].astype(F32) + zrecv[1, 3, slot, rows].astype(F32))
            xsend[slot, rows] = total.astype(BF16)
            return carry

        lax.fori_loop(0, 4, one, 0)
        for slot in range(4):
            stays = jnp.logical_and(xh == xl, q == slot)

            @pl.when(stays)
            def _():
                pltpu.make_async_copy(xsend.at[slot, rows], xrecv.at[x_source, rows], r_x.at[group]).start()

            @pl.when(jnp.logical_not(stays))
            def _():
                remote(
                    xsend.at[slot, rows], xrecv.at[x_source, rows], s_x, r_x.at[group], (x_section, y * 4 + slot)
                ).start()

    ended = {"adam": 0}

    def xlast(group):
        rows = rows_of(group)
        wait_bytes(xrecv.at[:, rows], r_x.at[group])
        for col in range(2):
            total = xrecv[col, rows].astype(F32) + xrecv[2 + col, rows].astype(F32)
            o_in[rows, col * W : (col + 1) * W] = total.astype(BF16)

    def adam(half):
        for k in range(2):
            wait_bytes(yrecv.at[0, 0, part_rows(0)], r_y.at[half, 3, k])
        ended["adam"] += 1
        if ended["adam"] == 1:
            for load in loads[4:]:
                load.wait()
        rows = part_rows(half)
        cols = slice(half * 128, half * 128 + 128)
        gradient = jnp.transpose(gsum[y, rows] + (yrecv[0, 3, rows].astype(F32) + yrecv[1, 3, rows].astype(F32)))
        was = mas_v[:, cols]
        first_new = BETA_ONE * m1_v[:, cols] + (1.0 - BETA_ONE) * gradient
        second_new = BETA_TWO * m2_v[:, cols] + (1.0 - BETA_TWO) * gradient * gradient
        direction = (
            first_new / (1.0 - BETA_ONE**STEP) / (jnp.sqrt(second_new / (1.0 - BETA_TWO**STEP)) + ADAM_EPS)
        )
        updated = was - LEARN_RATE * (direction + DECAY_RATE * was)
        wn[y, half] = updated.astype(BF16)
        for k in range(2):
            gather_send(wn.at[:, half], s_n, r_n.at[half], 0, k)
        o_master[0, :, cols] = updated
        o_m1[0, :, cols] = first_new
        o_m2[0, :, cols] = second_new

    def next(half, off):
        block = ring(y, off)
        part = jnp.dot(hid[block].reshape(4 * TOK, W), wn[block, half], preferred_element_type=F32)
        part = part.reshape(4, TOK, 128)
        kvn[half] = part if off == 0 else kvn[half] + part

    def share(half):
        remote(kvn.at[half, mates[2]], knc.at[half], s_kc, r_kc.at[half], mate_dev(mates[0])).start()
        remote(kvn.at[half, mates[0]], knr.at[half], s_kc, r_k.at[half], mate_dev(mates[0])).start()

    def cross(half):
        wait_bytes(knc.at[half], r_kc.at[half])
        kvs[half] = (kvn[half, mates[1]] + knc[half]).astype(BF16)
        remote(kvs.at[half], kns.at[half], s_k, r_k.at[half], mate_dev(mates[1])).start()

    def finish(half):
        wait_bytes(xa.at[0, pl.ds(0, 3), rows_of(0)], r_k.at[half])
        total = (kvn[half, q] + knr[half]) + kns[half].astype(F32)
        o_kv[0, :, half * 128 : half * 128 + 128] = total

    takes = {
        "relay": relay, "prepare": prepare, "old": old, "new": new, "arrive": arrive, "back": back, "grad": grad, "project": project,
        "put": put, "get": get, "ysum": ysum, "zsum": zsum, "zlast": zlast, "xlast": xlast, "adam": adam,
        "next": next, "share": share, "cross": cross, "finish": finish,
    }
    for name, *where in STEPS:
        with part_of(name + "_".join(str(n) for n in where)):
            takes[name](*where)

    with part_of("sent"):
        wait_bytes(xa.at[pl.ds(0, 6)], s_acts)
        wait_bytes(kvb.at[pl.ds(0, 3)], s_kv)
        wait_bytes(rmb.at[pl.ds(0, 3)], s_rm)
        wait_bytes(mrecv, s_m)
        wait_bytes(wt.at[pl.ds(0, 7)], s_w)
        wait_bytes(wn.at[pl.ds(0, 7)], s_n)
        wait_bytes(wt.at[pl.ds(0, 7)], s_y)
        wait_bytes(hid.at[pl.ds(0, 7)], s_z)
        wait_bytes(kvn.at[0], s_kc)
        wait_bytes(kvs, s_k)

        @pl.when(xh == xl)
        def _():
            wait_bytes(xsend.at[pl.ds(0, 3)], s_x)

        @pl.when(xh != xl)
        def _():
            wait_bytes(xsend, s_x)


def write_out(*refs):
    sources, targets, done = refs[:5], refs[5:10], refs[10]
    copies = [pltpu.make_async_copy(sources[i], targets[i], done.at[i]) for i in range(5)]
    for copy in copies:
        copy.start()
    for copy in copies:
        copy.wait()


def per_device(acts, gain, kv_grad, master, moment_one, moment_two):
    anywhere = pl.BlockSpec(memory_space=pl.ANY)
    vmem = pltpu.VMEM
    dma = pltpu.SemaphoreType.DMA
    rows = jax.ShapeDtypeStruct((1, W, W), F32)
    scratch = [
        vmem((TOK, D), BF16),
        vmem((1, D), F32),
        vmem((W, W), F32), vmem((W, W), F32), vmem((W, W), F32),
        vmem((N, 4, TOK, W), BF16),
        vmem((4, TOK, W), BF16),
        vmem((W, 4 * TOK), BF16),
        vmem((4, 8, 128), F32),
        vmem((4, TOK, 128), F32),
        vmem((N, W, W), BF16), vmem((N, 2, W, 128), BF16),
        vmem((N, 4, TOK, W), BF16),
        vmem((N, 4, TOK, W), F32),
        vmem((4, TOK, 128), F32),
        vmem((len(GROUPS), 8, 128), F32),
        vmem((len(GROUPS), 3, 8, 128), F32),
        vmem((4, TOK, 128), F32),
        vmem((N, W, W), F32),
        vmem((2, 4, W, W), BF16), vmem((2, 4, W, W), BF16),
        vmem((2, 4, 4, TOK, W), BF16), vmem((2, 4, 4, TOK, W), BF16),
        vmem((4, TOK, W), BF16), vmem((4, TOK, W), BF16),
        vmem((2, 4, TOK, 128), F32), vmem((2, TOK, 128), BF16),
        vmem((2, TOK, 128), F32), vmem((2, TOK, 128), F32), vmem((2, TOK, 128), BF16),
        dma((6,)), dma,
        dma, dma, dma, dma, dma, dma, dma, dma, dma, dma, dma,
        dma((len(SETS),)), dma((3,)), dma, dma((len(GROUPS),)),
        dma((4, 2)), dma((2, 4, 2)), dma((2, 4, 2)), dma((32,)),
        dma((len(GROUPS),)), dma((2,)), dma((2,)),
    ]
    shapes = (
        rows, rows, rows,
        jax.ShapeDtypeStruct((TOK, 2 * W), BF16),
        jax.ShapeDtypeStruct((1, TOK, W), F32),
    )
    given = [
        pltpu.with_memory_space_constraint(a, pltpu.HBM)
        for a in (acts, gain, kv_grad, master, moment_one, moment_two)
    ]
    results = pl.pallas_call(
        kernel,
        out_shape=tuple(vmem(shape.shape, shape.dtype) for shape in shapes),
        in_specs=[pl.BlockSpec(memory_space=pltpu.HBM)] * 6,
        out_specs=(pl.BlockSpec(memory_space=pltpu.VMEM),) * 5,
        scratch_shapes=scratch,
        compiler_params=pltpu.CompilerParams(
            collective_id=0, has_side_effects=True, vmem_limit_bytes=VMEM_BYTES
        ),
        cost_estimate=pl.CostEstimate(flops=1_700_000_000, bytes_accessed=6_000_000, transcendentals=200_000),
    )(*given)
    return pl.pallas_call(
        write_out,
        out_shape=shapes,
        in_specs=[pl.BlockSpec(memory_space=pltpu.VMEM)] * 5,
        out_specs=(anywhere,) * 5,
        scratch_shapes=[dma((5,))],
        cost_estimate=pl.CostEstimate(flops=0, bytes_accessed=2_100_000, transcendentals=0),
    )(*[pltpu.with_memory_space_constraint(a, pltpu.VMEM) for a in results])


def solution(mesh):
    placed = (
        P("section", "dp", None),
        P("section", None),
        P("section", "dp", None),
        P("section", "dp", None),
        P("section", "dp", None),
        P("section", "dp", None),
    )
    return jax.shard_map(
        per_device,
        mesh=mesh,
        in_specs=placed,
        out_specs=(
            P("section", "dp", None),
            P("section", "dp", None),
            P("section", "dp", None),
            P("dp", "section"),
            P("section", "dp", None),
        ),
        check_vma=False,
    )
```

```python
import contextlib

import jax
import jax.numpy as jnp
from jax import lax
from jax.experimental import pallas as pl
from jax.experimental.pallas import tpu as pltpu
from jax.sharding import PartitionSpec as P

STEP = 20
NORM_EPS = 1e-05
ADAM_EPS = 1e-08
BETA_ONE = 0.9
BETA_TWO = 0.95
LEARN_RATE = 0.00015
DECAY_RATE = 0.1

F32 = jnp.float32
BF16 = jnp.bfloat16
MESH = pl.DeviceIdType.MESH
N = 8
D = 8192
TOK = 128
W = 256
VMEM_BYTES = 48 * 1024 * 1024
GROUPS = ((0, 64), (64, 32), (96, 32))
SETS = (
    (0, 0), (0, 7), (0, 1), (0, 2), (0, 6), (0, 5), (0, 3), (0, 4),
    (1, 4), (2, 4), (1, 3), (2, 3), (1, 5), (2, 5), (1, 2), (1, 6),
    (2, 6), (2, 2), (1, 7), (2, 7), (1, 1), (2, 1), (1, 0), (2, 0),
)
AHEAD = 5
HOLD = 24
STEPS = (
    ("relay",), ("old", 1, 0), ("old", 1, 1), ("prepare",), ("arrive", 0), ("arrive", 1), ("project", 0),
    ("back", 0, 0), ("project", 1), ("arrive", 2), ("back", 0, 1), ("old", 2, 0), ("project", 7), ("back", 0, 7),
    ("arrive", 3), ("old", 2, 1), ("project", 2), ("back", 0, 2), ("project", 6), ("arrive", 4), ("back", 0, 6),
    ("arrive", 5), ("old", 3, 0), ("arrive", 6), ("old", 3, 1), ("project", 3), ("back", 0, 3), ("project", 5),
    ("back", 0, 5), ("arrive", 7), ("arrive", 8), ("arrive", 9), ("grad", 4), ("ysum", 0, 0, 1), ("ysum", 1, 0, 1),
    ("old", 4, 0), ("project", 4), ("back", 0, 4), ("put", 0), ("back", 1, 4), ("back", 2, 4), ("arrive", 10),
    ("back", 1, 3), ("arrive", 11), ("back", 2, 3), ("grad", 3), ("arrive", 12), ("back", 1, 5), ("arrive", 13),
    ("back", 2, 5), ("grad", 5), ("ysum", 0, 1, 0), ("ysum", 1, 1, 0), ("arrive", 14), ("ysum", 0, 1, 1),
    ("back", 1, 2), ("get", 0), ("zsum", 0, 0, 1, 0), ("zsum", 0, 0, 1, 1), ("zsum", 0, 1, 0, 0),
    ("zsum", 0, 1, 0, 1), ("ysum", 1, 1, 1), ("arrive", 15), ("back", 1, 6), ("arrive", 16), ("back", 2, 6),
    ("grad", 6), ("arrive", 17), ("back", 2, 2), ("grad", 2), ("ysum", 0, 2, 0), ("arrive", 18), ("back", 1, 7),
    ("zsum", 0, 1, 1, 0), ("ysum", 1, 2, 0), ("arrive", 19), ("back", 2, 7), ("grad", 7), ("zsum", 0, 1, 1, 1),
    ("ysum", 0, 2, 1), ("arrive", 20), ("back", 1, 1), ("zsum", 0, 2, 0, 0), ("arrive", 21), ("ysum", 1, 2, 1),
    ("back", 2, 1), ("grad", 1), ("zsum", 0, 2, 0, 1), ("arrive", 22), ("back", 1, 0), ("put", 1), ("ysum", 0, 3, 0),
    ("arrive", 23), ("back", 2, 0), ("put", 2), ("grad", 0), ("ysum", 1, 3, 0), ("zsum", 0, 2, 1, 0),
    ("ysum", 0, 3, 1), ("zsum", 0, 2, 1, 1), ("ysum", 1, 3, 1), ("zsum", 0, 3, 0, 0), ("get", 1),
    ("zsum", 1, 0, 1, 0), ("zsum", 1, 1, 0, 0), ("zsum", 0, 3, 0, 1), ("get", 2), ("zsum", 2, 0, 1, 0),
    ("zsum", 2, 1, 0, 0), ("zsum", 0, 3, 1, 0), ("adam", 0), ("next", 0, 0), ("adam", 1), ("next", 1, 0),
    ("zsum", 1, 1, 1, 0), ("zsum", 0, 3, 1, 1), ("zsum", 1, 2, 0, 0), ("new", 0, 1, 0), ("zsum", 2, 1, 1, 0),
    ("new", 0, 1, 1), ("next", 0, 1), ("next", 0, 7), ("zsum", 2, 2, 0, 0), ("new", 1, 1, 0), ("new", 1, 1, 1),
    ("next", 1, 1), ("next", 1, 7), ("new", 0, 2, 0), ("zsum", 1, 2, 1, 0), ("zlast", 0), ("new", 0, 2, 1),
    ("next", 0, 2), ("next", 0, 6), ("zsum", 1, 3, 0, 0), ("new", 1, 2, 0), ("zsum", 2, 2, 1, 0), ("new", 1, 2, 1),
    ("next", 1, 2), ("next", 1, 6), ("zsum", 2, 3, 0, 0), ("new", 0, 3, 0), ("zsum", 1, 3, 1, 0), ("new", 0, 3, 1),
    ("next", 0, 3), ("next", 0, 5), ("new", 1, 3, 0), ("zsum", 2, 3, 1, 0), ("xlast", 0), ("new", 1, 3, 1),
    ("next", 1, 3), ("next", 1, 5), ("new", 0, 4, 0), ("next", 0, 4), ("share", 0), ("zlast", 1), ("cross", 0),
    ("new", 1, 4, 0), ("next", 1, 4), ("share", 1), ("zlast", 2), ("cross", 1), ("xlast", 1), ("finish", 0),
    ("xlast", 2), ("finish", 1),
)

def part_of(name):
    return contextlib.nullcontext()


def rows_of(group):
    return pl.ds(*GROUPS[group])


def part_rows(part):
    return pl.ds(part * 128, 128)


def wide(a):
    return jnp.concatenate([a, a], axis=-1)


def kernel(
    acts, gain, kv, master, mom1, mom2,
    o_master, o_m1, o_m2, o_in, o_kv,
    a_full, gain_v, mas_v, m1_v, m2_v,
    xa, kvb, kvt, rmb, invc, wt, wn, hid, sc, macc, msend, mrecv, mcol,
    gsum, ysend, yrecv, zsend, zrecv, xsend, xrecv, kvn, kvs, knc, knr, kns,
    l_in, l_acts, s_acts, s_kv, s_rm, s_m, s_w, s_n, s_y, s_z, s_x, s_k, s_kc,
    r_acts, r_kv, r_rm, r_m, r_w, r_n, r_y, r_z, r_x, r_k, r_kc,
):
    section = lax.axis_index("section")
    dp = lax.axis_index("dp")
    z = lax.div(section, 2)
    xh = lax.rem(section, 2)
    y = lax.div(dp, 4)
    q = lax.rem(dp, 4)
    xl = lax.div(q, 2)
    c = lax.rem(q, 2)
    mates = (xl * 2 + (1 - c), (1 - xl) * 2 + c, (1 - xl) * 2 + (1 - c))

    def ring(at, off):
        return lax.rem(at + off, N)

    def y_dev(off):
        return (section, ring(y, off) * 4 + q)

    def z_dev(off):
        return (ring(z, off) * 2 + xh, dp)

    def mate_dev(mate):
        return (section, y * 4 + mate)

    def remote(src, dst, send, recv, device):
        return pltpu.make_async_remote_copy(
            src_ref=src, dst_ref=dst, send_sem=send, recv_sem=recv, device_id=device, device_id_type=MESH
        )

    def wait_bytes(ref, sem):
        pltpu.make_async_copy(ref, ref, sem).wait()

    def columns(block):
        return pl.ds(pl.multiple_of(block * 1024 + q * W, W), W)

    barrier = pltpu.get_barrier_semaphore()
    for fh in range(2):
        for fl in range(2):
            for fc in range(2):
                if fh + fl + fc == 0:
                    continue
                other_h = 1 - xh if fh else xh
                other_l = 1 - xl if fl else xl
                other_c = 1 - c if fc else c
                device = (z * 2 + other_h, y * 4 + other_l * 2 + other_c)
                pl.semaphore_signal(barrier, inc=1, device_id=device, device_id_type=MESH)
    for device in (y_dev(1), y_dev(7), z_dev(1), z_dev(7)):
        pl.semaphore_signal(barrier, inc=1, device_id=device, device_id_type=MESH)

    loads = [
        pltpu.make_async_copy(kv.at[0], kvb.at[q], l_in.at[0]),
        pltpu.make_async_copy(master.at[0], mas_v, l_in.at[1]),
        pltpu.make_async_copy(acts.at[0], a_full, l_in.at[2]),
        pltpu.make_async_copy(gain, gain_v, l_in.at[3]),
        pltpu.make_async_copy(mom1.at[0], m1_v, l_in.at[4]),
        pltpu.make_async_copy(mom2.at[0], m2_v, l_in.at[5]),
    ]
    for load in loads:
        load.start()
    for off in range(N):
        block = ring(y, off)
        pltpu.make_async_copy(acts.at[0, :, columns(block)], xa.at[block, q], l_acts).start()

    with part_of("barrier"):
        pl.semaphore_wait(barrier, 11)

    def send_acts(k):
        group, off = SETS[k]
        rows = rows_of(group)
        block = ring(y, off)
        for mate in mates:
            source = acts.at[0, rows, pl.ds(pl.multiple_of(block * 1024 + mate * W, W), W)]
            remote(source, xa.at[block, q, rows], s_acts, r_acts.at[k], mate_dev(mate)).start()

    def kv_copy(which):
        slot, mate = ((q, mates[0]), (q, mates[1]), (mates[1], mates[0]))[which]
        return remote(kvb.at[slot], kvb.at[slot], s_kv, r_kv.at[which], mate_dev(mate))

    def gather_send(buffer, send, recv, hop, k):
        for way in range(2):
            block = ring(y, N - hop if way == 0 else hop)
            rows = buffer.at[block, part_rows(k if way == 0 else 1 - k)]
            remote(rows, rows, send, recv.at[hop, k], y_dev(1 if way == 0 else 7)).start()

    def gather_step(buffer, send, recv, hop, k):
        wait_bytes(buffer.at[0], recv.at[hop - 1, k])
        if hop < 3 or (hop == 3 and k == 0):
            gather_send(buffer, send, recv, hop, k)

    loads[0].wait()
    kv_copy(1).start()
    kv_copy(0).start()
    send_acts(0)
    send_acts(1)
    with part_of("wt"):
        loads[1].wait()
        wt[y] = jnp.transpose(mas_v[...]).astype(BF16)
    for k in range(2):
        gather_send(wt, s_w, r_w, 0, k)

    with part_of("squares"):
        loads[2].wait()

        def add_squares(step, total):
            part = a_full[:, pl.ds(pl.multiple_of(step * 512, 512), 512)].astype(F32)
            part = part * part
            return total + ((part[:, :128] + part[:, 128:256]) + (part[:, 256:384] + part[:, 384:]))

        squares = lax.fori_loop(0, 16, add_squares, jnp.zeros((TOK, 128), F32))
        mean_row = jnp.sum(jnp.transpose(squares), axis=0, keepdims=True) / D
        rmb[q] = jnp.broadcast_to(jnp.sqrt(mean_row + NORM_EPS), (8, 128))
    for mate in mates:
        remote(rmb.at[q], rmb.at[q], s_rm, r_rm, mate_dev(mate)).start()
    for k in range(2, min(AHEAD, HOLD)):
        send_acts(k)
    sent = [min(AHEAD, HOLD), False, -1]
    macc[...] = jnp.zeros_like(macc)
    loads[3].wait()
    wait_bytes(xa.at[pl.ds(0, 2)], l_acts)

    def relay():
        kv_copy(1).wait_recv()
        kv_copy(2).start()

    def prepare():
        kv_copy(0).wait_recv()
        kv_copy(2).wait_recv()
        wait_bytes(rmb.at[pl.ds(0, 3)], r_rm)

        def one(slot, carry):
            root = jnp.transpose(jnp.broadcast_to(rmb[slot][0:1, :], (128, 128)))
            invc[slot] = 1.0 / root
            return carry

        lax.fori_loop(0, 4, one, 0)
        for slot in range(4):
            kvt[:, slot * TOK : (slot + 1) * TOK] = jnp.transpose(kvb[slot].astype(F32)).astype(BF16)

    def old(hop, k):
        gather_step(wt, s_w, r_w, hop, k)

    def new(half, hop, k):
        gather_step(wn.at[:, half], s_n, r_n.at[half], hop, k)

    def feed(k):
        for later in range(sent[0], min(k + 1 + AHEAD, len(SETS) if sent[1] else HOLD)):
            send_acts(later)
            sent[0] = later + 1
        sent[2] = k

    def project(off):
        block = ring(y, off)
        product = jnp.dot(kvb[...].reshape(4 * TOK, W), wt[block], preferred_element_type=F32)
        sc[block] = (product * gain_v[:, columns(block)]).reshape(4, TOK, W)
        projected.add(off)

    projected = set()
    hidden_only = set()

    def features(group, off, hides, means):
        rows = rows_of(group)
        block = ring(y, off)
        gain_row = gain_v[:, columns(block)]

        def one(slot, carry):
            unit = xa[block, slot, rows, :].astype(F32) * wide(invc[slot, rows, :])
            if hides:
                hid[block, slot, rows, :] = (unit * gain_row).astype(BF16)
            if means:
                both = sc[block, slot, rows, :] * unit
                macc[slot, rows, :] += both[:, :128] + both[:, 128:]
            return carry

        lax.fori_loop(0, 4, one, 0)

    def arrive(k):
        group, off = SETS[k]
        wait_bytes(xa.at[0, pl.ds(0, 3), rows_of(group)], r_acts.at[k])
        feed(k)
        features(group, off, True, off in projected)
        if off not in projected:
            hidden_only.add((group, off))

    def back(group, off):
        if (group, off) in hidden_only:
            features(group, off, False, True)

    def grad(off):
        block = ring(y, off)
        gsum[block] = jnp.dot(kvt[...], hid[block].reshape(4 * TOK, W), preferred_element_type=F32)

    def put(group):
        rows = rows_of(group)
        slots = 128 // GROUPS[group][1]
        msend[group] = jnp.zeros((8, 128), F32)
        for row in range(4 // slots):
            both = macc[pl.ds(row * slots, slots), rows].reshape(128, 128)
            msend[group, row : row + 1, :] = jnp.sum(jnp.transpose(both), axis=0, keepdims=True)
        for r, mate in enumerate(mates):
            remote(msend.at[group], mrecv.at[group, r], s_m, r_m.at[group], mate_dev(mate)).start()
        sent[1] = True
        feed(sent[2])

    def get(group):
        wait_bytes(mrecv.at[group], r_m.at[group])
        total = ((msend[group] + mrecv[group, 0]) + (mrecv[group, 1] + mrecv[group, 2])) / D
        slots = 128 // GROUPS[group][1]
        for row in range(4 // slots):
            column = jnp.transpose(jnp.broadcast_to(total[row : row + 1, :], (128, 128)))
            mcol[pl.ds(row * slots, slots), rows_of(group)] = column.reshape(slots, GROUPS[group][1], 128)

    def branch(group, block, slot):
        rows = rows_of(group)
        inv = wide(invc[slot, rows, :])
        unit = xa[block, slot, rows, :].astype(F32) * inv
        return ((sc[block, slot, rows, :] - unit * wide(mcol[slot, rows])) * inv).astype(BF16)

    def ysum(half, step, k):
        adds = step > 1 or (step == 1 and k == 1)
        if adds:
            wait_bytes(yrecv.at[0, 0, part_rows(0)], r_y.at[half, step - 1, k])
        for way in range(2):
            part = way if k == 1 else 1 - way
            rows = pl.ds(half * 128 + part * 64, 64)
            total = gsum[ring(y, 4 - step if way == 0 else 4 + step), rows]
            if adds:
                total = total + yrecv[way, step - 1, rows].astype(F32)
            ysend[way, step, rows] = total.astype(BF16)
            remote(
                ysend.at[way, step, rows], yrecv.at[way, step, rows], s_y, r_y.at[half, step, k],
                y_dev(1 if way == 0 else 7),
            ).start()

    def z_sem(group, step, k, j):
        return r_z.at[step * 4 + k * 2 + j if group == 0 else 8 + group * 8 + step * 2 + k]

    z_bytes = zrecv.at[0, 0, pl.ds(0, 2), rows_of(0)]

    def zsum(group, step, k, j):
        rows = rows_of(group)
        slots = 1 if group == 0 else 2
        adds = step > 1 or (step == 1 and k == 1)
        if adds:
            wait_bytes(z_bytes, z_sem(group, step - 1, k, j))
        for way in range(2):
            first = 2 * (way if k == 1 else 1 - way) + j
            for slot in range(first, first + slots):
                own = branch(group, ring(z, 4 - step if way == 0 else 4 + step), slot)
                if adds:
                    own = (own.astype(F32) + zrecv[way, step - 1, slot, rows].astype(F32)).astype(BF16)
                zsend[way, step, slot, rows] = own
            part = pl.ds(first, slots)
            remote(
                zsend.at[way, step, part, rows], zrecv.at[way, step, part, rows], s_z, z_sem(group, step, k, j),
                z_dev(1 if way == 0 else 7),
            ).start()

    x_section = z * 2 + xl
    x_source = xh * 2 + c

    def zlast(group):
        rows = rows_of(group)
        for k in range(2):
            for j in range(2 if group == 0 else 1):
                wait_bytes(z_bytes, z_sem(group, 3, k, j))

        def one(slot, carry):
            total = branch(group, z, slot).astype(F32)
            total = total + (zrecv[0, 3, slot, rows].astype(F32) + zrecv[1, 3, slot, rows].astype(F32))
            xsend[slot, rows] = total.astype(BF16)
            return carry

        lax.fori_loop(0, 4, one, 0)
        for slot in range(4):
            stays = jnp.logical_and(xh == xl, q == slot)

            @pl.when(stays)
            def _():
                pltpu.make_async_copy(xsend.at[slot, rows], xrecv.at[x_source, rows], r_x.at[group]).start()

            @pl.when(jnp.logical_not(stays))
            def _():
                remote(
                    xsend.at[slot, rows], xrecv.at[x_source, rows], s_x, r_x.at[group], (x_section, y * 4 + slot)
                ).start()

    ended = {"adam": 0}

    def xlast(group):
        rows = rows_of(group)
        wait_bytes(xrecv.at[:, rows], r_x.at[group])
        for col in range(2):
            total = xrecv[col, rows].astype(F32) + xrecv[2 + col, rows].astype(F32)
            o_in[rows, col * W : (col + 1) * W] = total.astype(BF16)

    def adam(half):
        for k in range(2):
            wait_bytes(yrecv.at[0, 0, part_rows(0)], r_y.at[half, 3, k])
        ended["adam"] += 1
        if ended["adam"] == 1:
            for load in loads[4:]:
                load.wait()
        rows = part_rows(half)
        cols = slice(half * 128, half * 128 + 128)
        gradient = jnp.transpose(gsum[y, rows] + (yrecv[0, 3, rows].astype(F32) + yrecv[1, 3, rows].astype(F32)))
        was = mas_v[:, cols]
        first_new = BETA_ONE * m1_v[:, cols] + (1.0 - BETA_ONE) * gradient
        second_new = BETA_TWO * m2_v[:, cols] + (1.0 - BETA_TWO) * gradient * gradient
        direction = (
            first_new / (1.0 - BETA_ONE**STEP) / (jnp.sqrt(second_new / (1.0 - BETA_TWO**STEP)) + ADAM_EPS)
        )
        updated = was - LEARN_RATE * (direction + DECAY_RATE * was)
        wn[y, half] = updated.astype(BF16)
        for k in range(2):
            gather_send(wn.at[:, half], s_n, r_n.at[half], 0, k)
        o_master[0, :, cols] = updated
        o_m1[0, :, cols] = first_new
        o_m2[0, :, cols] = second_new

    def next(half, off):
        block = ring(y, off)
        part = jnp.dot(hid[block].reshape(4 * TOK, W), wn[block, half], preferred_element_type=F32)
        part = part.reshape(4, TOK, 128)
        kvn[half] = part if off == 0 else kvn[half] + part

    def share(half):
        remote(kvn.at[half, mates[2]], knc.at[half], s_kc, r_kc.at[half], mate_dev(mates[0])).start()
        remote(kvn.at[half, mates[0]], knr.at[half], s_kc, r_k.at[half], mate_dev(mates[0])).start()

    def cross(half):
        wait_bytes(knc.at[half], r_kc.at[half])
        kvs[half] = (kvn[half, mates[1]] + knc[half]).astype(BF16)
        remote(kvs.at[half], kns.at[half], s_k, r_k.at[half], mate_dev(mates[1])).start()

    def finish(half):
        wait_bytes(xa.at[0, pl.ds(0, 3), rows_of(0)], r_k.at[half])
        total = (kvn[half, q] + knr[half]) + kns[half].astype(F32)
        o_kv[0, :, half * 128 : half * 128 + 128] = total

    takes = {
        "relay": relay, "prepare": prepare, "old": old, "new": new, "arrive": arrive, "back": back, "grad": grad, "project": project,
        "put": put, "get": get, "ysum": ysum, "zsum": zsum, "zlast": zlast, "xlast": xlast, "adam": adam,
        "next": next, "share": share, "cross": cross, "finish": finish,
    }
    for name, *where in STEPS:
        with part_of(name + "_".join(str(n) for n in where)):
            takes[name](*where)

    with part_of("sent"):
        wait_bytes(xa.at[pl.ds(0, 6)], s_acts)
        wait_bytes(kvb.at[pl.ds(0, 3)], s_kv)
        wait_bytes(rmb.at[pl.ds(0, 3)], s_rm)
        wait_bytes(mrecv, s_m)
        wait_bytes(wt.at[pl.ds(0, 7)], s_w)
        wait_bytes(wn.at[pl.ds(0, 7)], s_n)
        wait_bytes(wt.at[pl.ds(0, 7)], s_y)
        wait_bytes(hid.at[pl.ds(0, 7)], s_z)
        wait_bytes(kvn.at[0], s_kc)
        wait_bytes(kvs, s_k)

        @pl.when(xh == xl)
        def _():
            wait_bytes(xsend.at[pl.ds(0, 3)], s_x)

        @pl.when(xh != xl)
        def _():
            wait_bytes(xsend, s_x)


def write_out(*refs):
    sources, targets, done = refs[:5], refs[5:10], refs[10]
    copies = [pltpu.make_async_copy(sources[i], targets[i], done.at[i]) for i in range(5)]
    for copy in copies:
        copy.start()
    for copy in copies:
        copy.wait()


def per_device(acts, gain, kv_grad, master, moment_one, moment_two):
    anywhere = pl.BlockSpec(memory_space=pl.ANY)
    vmem = pltpu.VMEM
    dma = pltpu.SemaphoreType.DMA
    rows = jax.ShapeDtypeStruct((1, W, W), F32)
    scratch = [
        vmem((TOK, D), BF16),
        vmem((1, D), F32),
        vmem((W, W), F32), vmem((W, W), F32), vmem((W, W), F32),
        vmem((N, 4, TOK, W), BF16),
        vmem((4, TOK, W), BF16),
        vmem((W, 4 * TOK), BF16),
        vmem((4, 8, 128), F32),
        vmem((4, TOK, 128), F32),
        vmem((N, W, W), BF16), vmem((N, 2, W, 128), BF16),
        vmem((N, 4, TOK, W), BF16),
        vmem((N, 4, TOK, W), F32),
        vmem((4, TOK, 128), F32),
        vmem((len(GROUPS), 8, 128), F32),
        vmem((len(GROUPS), 3, 8, 128), F32),
        vmem((4, TOK, 128), F32),
        vmem((N, W, W), F32),
        vmem((2, 4, W, W), BF16), vmem((2, 4, W, W), BF16),
        vmem((2, 4, 4, TOK, W), BF16), vmem((2, 4, 4, TOK, W), BF16),
        vmem((4, TOK, W), BF16), vmem((4, TOK, W), BF16),
        vmem((2, 4, TOK, 128), F32), vmem((2, TOK, 128), BF16),
        vmem((2, TOK, 128), F32), vmem((2, TOK, 128), F32), vmem((2, TOK, 128), BF16),
        dma((6,)), dma,
        dma, dma, dma, dma, dma, dma, dma, dma, dma, dma, dma,
        dma((len(SETS),)), dma((3,)), dma, dma((len(GROUPS),)),
        dma((4, 2)), dma((2, 4, 2)), dma((2, 4, 2)), dma((32,)),
        dma((len(GROUPS),)), dma((2,)), dma((2,)),
    ]
    shapes = (
        rows, rows, rows,
        jax.ShapeDtypeStruct((TOK, 2 * W), BF16),
        jax.ShapeDtypeStruct((1, TOK, W), F32),
    )
    given = [
        pltpu.with_memory_space_constraint(a, pltpu.HBM)
        for a in (acts, gain, kv_grad, master, moment_one, moment_two)
    ]
    results = pl.pallas_call(
        kernel,
        out_shape=tuple(vmem(shape.shape, shape.dtype) for shape in shapes),
        in_specs=[pl.BlockSpec(memory_space=pltpu.HBM)] * 6,
        out_specs=(pl.BlockSpec(memory_space=pltpu.VMEM),) * 5,
        scratch_shapes=scratch,
        compiler_params=pltpu.CompilerParams(
            collective_id=0, has_side_effects=True, vmem_limit_bytes=VMEM_BYTES
        ),
        cost_estimate=pl.CostEstimate(flops=1_700_000_000, bytes_accessed=6_000_000, transcendentals=200_000),
    )(*given)
    return pl.pallas_call(
        write_out,
        out_shape=shapes,
        in_specs=[pl.BlockSpec(memory_space=pltpu.VMEM)] * 5,
        out_specs=(anywhere,) * 5,
        scratch_shapes=[dma((5,))],
        cost_estimate=pl.CostEstimate(flops=0, bytes_accessed=2_100_000, transcendentals=0),
    )(*[pltpu.with_memory_space_constraint(a, pltpu.VMEM) for a in results])


def solution(mesh):
    placed = (
        P("section", "dp", None),
        P("section", None),
        P("section", "dp", None),
        P("section", "dp", None),
        P("section", "dp", None),
        P("section", "dp", None),
    )
    return jax.shard_map(
        per_device,
        mesh=mesh,
        in_specs=placed,
        out_specs=(
            P("section", "dp", None),
            P("section", "dp", None),
            P("section", "dp", None),
            P("dp", "section"),
            P("section", "dp", None),
        ),
        check_vma=False,
    )
```
